32 devices in a mesh: win: 2 (over y), pair: 4 (over z), stk: 2 (over x), lag: 2 (over core).
Axes of the slice: x: 2, y: 2, z: 4, core: 2. Of those that a mesh axis runs over, the one named last changes fastest.
Arguments:
- spectra: bfloat16 [32, 4, 256, 1024], P('win', 'pair', 'stk'), parts along dimension 0, may hold values from -40 to 40
- pair_blocks: int32 [8, 40, 2], P('win'), parts along dimension 0, may hold values from 0 to 63, as said below
- live_pairs: int32 [8], P('win'), parts along dimension 0, may hold values from 10 to 40, as said below
- stack_group: int32 [8, 40], P('win'), parts along dimension 0, may hold values from 0 to 3, as said below
Outputs:
- stacks: float32 [8, 256, 1024], P('win', 'stk', ('pair', 'lag')), parts along dimension 0
The draws below stay inside these ranges and needn't reach their ends.
There are 2 independent parts, one for each index of `win`. The reference program is written for one: setup_inputs(seed, part) draws one part's arguments, and reference() takes and returns one part's arrays. A program takes and returns all parts, laid end to end along the dimension named above; each array names one. Nothing has to cross between parts.
Inputs may be any that keep to these rules, and one draw needn't show every extreme that they name: `pair_blocks`: every pair names a first block and a second block 1 to 8 higher. The pairs of all 40 slots of one owner span exactly 32 consecutive blocks, from the smallest first block to the largest second block. An owner's first live_pairs slots are used, the rest are not. Some owner uses all 40. `stack_group`: in the first 4 slots of every owner each group stands once.
All inputs are finite; a program needn't handle non-finite values.
Results may differ from the reference program's by a relative error of at most 0.0058.
Values may be sent and summed in bfloat16 or wider, within the bound.
A program may use at most 128 MiB of HBM per device.

```python
import math
import jax
import jax.numpy as jnp
from jax import lax

FREQ = 512
CH_BLK = 256
NBLK = 64
WINB = 32
MAXOFF = 8
PB_DEV = 40
NGRP = 4
HW = 15
BLK_DEV = 16
N_PAIR = 4


def draw_spectra(key, part):
    shape_full = (BLK_DEV, N_PAIR, CH_BLK, 2 * FREQ)
    scale_key, noise_key = jax.random.split(key, 2)
    channel_scale = jnp.exp(jax.random.uniform(scale_key, (BLK_DEV, N_PAIR, CH_BLK, 1), jnp.float32, 0.0, math.log(10.0)))
    values = channel_scale * jax.random.truncated_normal(noise_key, -4.0, 4.0, shape_full, jnp.float32)
    return values.astype(jnp.bfloat16)


def owner_plan(key):
    plan_key = jax.random.fold_in(key, 4242)
    start_key, pick_key, live_key, full_key, group_key, cycle_key = jax.random.split(plan_key, 6)
    edge_key = jax.random.fold_in(plan_key, 77)
    low_key, step_key = jax.random.split(edge_key)
    choices_total = (WINB - MAXOFF) * MAXOFF
    starts = jax.random.randint(start_key, (N_PAIR,), 0, NBLK - WINB + 1)
    low_owner = jax.random.randint(low_key, (), 0, N_PAIR)
    high_owner = (low_owner + jax.random.randint(step_key, (), 1, N_PAIR)) % N_PAIR
    owner_ids = jnp.arange(N_PAIR)
    starts = jnp.where(owner_ids == low_owner, 0, starts)
    starts = jnp.where(owner_ids == high_owner, NBLK - WINB, starts)

    def pick_slots(owner_key):
        middle_key, order_key = jax.random.split(owner_key)
        middle = jax.random.permutation(middle_key, choices_total - 2) + 1
        chosen = jnp.concatenate([jnp.array([0, choices_total - 1], jnp.int32), middle[:PB_DEV - 2].astype(jnp.int32)])
        return jax.random.permutation(order_key, chosen)
    picked = jax.vmap(pick_slots)(jax.random.split(pick_key, N_PAIR))
    first_block = starts[:, None] + picked // MAXOFF
    second_block = first_block + picked % MAXOFF + 1
    pair_blocks = jnp.stack([first_block, second_block], axis=-1).astype(jnp.int32)
    halving = jax.random.randint(live_key, (N_PAIR,), 0, 4)
    live_counts = jnp.maximum(PB_DEV // 4, PB_DEV // jnp.left_shift(1, halving))
    busiest = jax.random.randint(full_key, (), 0, N_PAIR)
    live_counts = jnp.where(jnp.arange(N_PAIR) == busiest, PB_DEV, live_counts).astype(jnp.int32)
    groups = jax.random.randint(group_key, (N_PAIR, PB_DEV), 0, NGRP)
    cycle_shift = jax.random.randint(cycle_key, (N_PAIR, 1), 0, NGRP)
    slot_ids = jnp.arange(PB_DEV)[None, :]
    groups = jnp.where(slot_ids < NGRP, (slot_ids + cycle_shift) % NGRP, groups).astype(jnp.int32)
    return (pair_blocks, live_counts, groups)


def draw_pair_blocks(key, part):
    return owner_plan(key)[0]


def draw_live_pairs(key, part):
    return owner_plan(key)[1]


def draw_stack_group(key, part):
    return owner_plan(key)[2]


def setup_inputs(seed: int = 0, part: int = 0) -> dict:
    seeds = jax.random.split(jax.random.key(seed), 5)
    own_keys = jax.random.split(jax.random.fold_in(seeds[4], part), 5)
    return {
        "spectra": draw_spectra(jax.random.fold_in(jax.random.fold_in(seeds[4], part), 71), part),
        "pair_blocks": draw_pair_blocks(jax.random.fold_in(jax.random.fold_in(seeds[4], part), 71), part),
        "live_pairs": draw_live_pairs(jax.random.fold_in(jax.random.fold_in(seeds[4], part), 71), part),
        "stack_group": draw_stack_group(jax.random.fold_in(jax.random.fold_in(seeds[4], part), 71), part),
    }


AMP_FLOOR = 0.5
EPSILON = 1e-06

def lag_table(lag_ids, num_bins):
    bin_index = jnp.arange(num_bins, dtype=jnp.int32)[:, None]
    phase_turns = bin_index * (lag_ids[None, :] + num_bins) % (2 * num_bins)
    angles = phase_turns.astype(jnp.float32) * (math.pi / num_bins)
    cosine = jnp.cos(angles)
    sine_part = jnp.sin(angles)
    amp_scale = math.sqrt(2.0 / num_bins)
    upper_rows = jnp.concatenate([cosine, sine_part], axis=1)
    lower_rows = jnp.concatenate([-sine_part, cosine], axis=1)
    return (jnp.concatenate([upper_rows, lower_rows], axis=0) * amp_scale).astype(jnp.bfloat16)

def whiten_blocks(spectra):
    values = spectra.astype(jnp.float32)
    channel_power = lax.optimization_barrier(jnp.mean(values * values, axis=-1, keepdims=True)) * 2.0
    return (values / jnp.sqrt(channel_power + EPSILON)).astype(jnp.bfloat16)

def cross_spectra(first_spec, second_spec, num_bins):
    first_spec = first_spec.astype(jnp.float32)
    second_spec = second_spec.astype(jnp.float32)
    real_a = first_spec[..., :num_bins]
    imag_a = first_spec[..., num_bins:]
    real_b = second_spec[..., :num_bins]
    imag_b = second_spec[..., num_bins:]
    real_part = real_a * real_b + imag_a * imag_b
    imag_part = imag_a * real_b - real_a * imag_b
    return jnp.concatenate([real_part, imag_part], axis=-1).astype(jnp.bfloat16)

def phase_terms(correlation, half_lags):
    direct = correlation[:, :half_lags]
    quadrature = correlation[:, half_lags:]
    divisor = jnp.maximum(jnp.sqrt(direct * direct + quadrature * quadrature), AMP_FLOOR)
    return jnp.stack([direct, direct / divisor, quadrature / divisor], axis=1)

def reference(spectra, pair_blocks, live_pairs, stack_group):
    num_bins = FREQ
    channels = CH_BLK
    lag_count = 2 * num_bins
    whitened = whiten_blocks(spectra).reshape(NBLK, channels, 2 * num_bins)
    table_all = lag_table(jnp.arange(lag_count, dtype=jnp.int32), num_bins)
    slot_index = jnp.arange(PB_DEV, dtype=jnp.int32)
    group_index = jnp.arange(NGRP, dtype=jnp.int32)

    def owner_step(group_sums, inputs):
        owner_pairs, owner_live, owner_groups = inputs
        first_spec = jnp.take(whitened, owner_pairs[:, 0].astype(jnp.int32), axis=0)
        second_spec = jnp.take(whitened, owner_pairs[:, 1].astype(jnp.int32), axis=0)
        cross_rows = cross_spectra(first_spec, second_spec, num_bins).reshape(PB_DEV * channels, 2 * num_bins)
        correlation = jnp.dot(cross_rows, table_all, preferred_element_type=jnp.float32)
        phase_rows = phase_terms(correlation, lag_count).reshape(PB_DEV, channels * 3 * lag_count)
        weights = ((owner_groups[:, None] == group_index[None, :]) & (slot_index < owner_live)[:, None]).astype(jnp.float32)
        return (group_sums + jnp.dot(weights.T, phase_rows, precision=lax.Precision.HIGHEST), None)
    initial = jnp.zeros((NGRP, channels * 3 * lag_count), jnp.float32)
    group_sums, unused = lax.scan(owner_step, initial, (pair_blocks, live_pairs, stack_group))
    group_sums = group_sums.reshape(NGRP, channels, 3, lag_count)
    live_mask = slot_index[None, :] < live_pairs[:, None]
    member = (stack_group[:, :, None] == group_index[None, None, :]) & live_mask[:, :, None]
    members = lax.optimization_barrier(jnp.sum(member.astype(jnp.float32), axis=(0, 1)))
    norm_root = jnp.sqrt(members)[:, None, None]
    linear = group_sums[:, :, 0] / norm_root
    coherence = jnp.sqrt(group_sums[:, :, 1] * group_sums[:, :, 1] + group_sums[:, :, 2] * group_sums[:, :, 2]) / norm_root
    padded = jnp.pad(coherence, ((0, 0), (0, 0), (HW, HW)))
    smoothed = jnp.zeros_like(coherence)
    for offset_tap in range(2 * HW + 1):
        smoothed = smoothed + padded[:, :, offset_tap:offset_tap + lag_count]
    smoothed = smoothed / (2 * HW + 1)
    return linear * smoothed * smoothed
```

```python
import functools
import math

import jax
import jax.numpy as jnp
import numpy as np
from jax import lax
from jax.experimental import pallas as pl
from jax.experimental.pallas import tpu as pltpu
from jax.sharding import PartitionSpec as P

NGRP = 4
HW = 15
AMP_FLOOR = 0.5
EPSILON = 1e-06
ROWS = 16
BATCH = 16
QUAD = 4
CHUNKS = 4
COLS = 128
CHUNK_ROWS = 4
PARTS = 2


def tables(num_bins):
    bins = np.arange(num_bins)[:, None]
    steps = np.arange(num_bins)[None, :]
    angles = (bins * steps % (2 * num_bins)) * (math.pi / num_bins)
    scale = math.sqrt(2.0 / num_bins)
    cosine = np.cos(angles) * scale
    sine = np.sin(angles) * scale
    upper = np.concatenate([cosine, sine], axis=1)
    lower = np.concatenate([-sine, cosine], axis=1)
    even = np.concatenate([upper[0::2], lower[0::2]], axis=0)
    odd = np.concatenate([upper[1::2], lower[1::2]], axis=0)
    shape = (num_bins, 2, num_bins // COLS, COLS)
    even, odd = (t.reshape(shape).swapaxes(1, 2).reshape(t.shape) for t in (even, odd))
    return tuple(jnp.asarray(t, jnp.bfloat16) for t in (even, odd))


def bin_order(bins):
    row = lax.broadcasted_iota(jnp.int32, (bins, bins), 0)
    col = lax.broadcasted_iota(jnp.int32, (bins, bins), 1)
    place = jnp.where(col < bins // 2, 2 * col, 2 * col - (bins - 1))
    return jnp.where(row == place, 1.0, 0.0).astype(jnp.bfloat16)


def kernel(
    pairs, live, groups, white, even_ref, odd_ref, out_ref,
    cross, acc, first_ids, second_ids, quad_at, quad_group, counts,
):
    owners = live.shape[0]
    blocks, (_, rows, width) = white.shape[0] - 1, white.shape
    bins = width // 2
    half = bins // 2

    stride = (first_ids.shape[0] - QUAD) // NGRP

    def add_owner(q, carry):
        def add_slot(s, carry):
            group = groups[q, s]
            count = counts[group]
            at = group * stride + count
            first_ids[at] = pairs[q, 0, s]
            second_ids[at] = pairs[q, 1, s]
            counts[group] = count + 1
            return carry

        return lax.fori_loop(0, live[q], add_slot, carry)

    for g in range(NGRP):
        counts[g] = 0
    lax.fori_loop(0, owners, add_owner, 0)

    def blank(at):
        for i in range(QUAD):
            first_ids[at + i] = blocks
            second_ids[at + i] = blocks

    total = 0
    for g in range(NGRP):
        blank(g * stride + counts[g])

        def add_quad(n, total, g=g):
            quad_at[total] = g * stride + n * QUAD
            quad_group[total] = g
            return total + 1

        total = lax.fori_loop(0, pl.cdiv(counts[g], QUAD), add_quad, total)
    blank(NGRP * stride)
    for i in range(BATCH // QUAD):
        quad_at[total + i] = NGRP * stride
        quad_group[total + i] = 0

    acc[...] = jnp.zeros_like(acc)

    def add_batch(step, carry):
        base = step * (BATCH // QUAD)
        for i in range(BATCH):
            at = quad_at[base + i // QUAD] + i % QUAD
            first = white[first_ids[at]].astype(jnp.float32)
            second = white[second_ids[at]].astype(jnp.float32)
            for n in range(2):
                lo, mid, hi = 2 * n * half, (2 * n + 1) * half, (2 * n + 2) * half
                ra, ia = first[:, lo:mid], first[:, mid:hi]
                rb, ib = second[:, lo:mid], second[:, mid:hi]
                cross[i * rows : (i + 1) * rows, lo:mid] = (ra * rb + ia * ib).astype(jnp.bfloat16)
                cross[i * rows : (i + 1) * rows, mid:hi] = (ia * rb - ra * ib).astype(jnp.bfloat16)
        for col in range(0, bins, COLS):
            def product(n, table):
                both = jnp.dot(
                    cross[:, n * bins : (n + 1) * bins],
                    table[:, 2 * col : 2 * (col + COLS)],
                    preferred_element_type=jnp.float32,
                )
                return both[:, :COLS], both[:, COLS:]

            even_d, even_q = product(0, even_ref)
            odd_d, odd_q = product(1, odd_ref)
            for u in range(BATCH // QUAD):
                start = pl.multiple_of(quad_group[base + u] * rows, rows)
                for side, at in ((-1, col), (1, bins + col)):
                    sums = [0.0, 0.0, 0.0]
                    for i in range(u * QUAD, (u + 1) * QUAD):
                        cut = slice(i * rows, (i + 1) * rows)
                        if side < 0:
                            direct, quad = even_d[cut] - odd_d[cut], even_q[cut] - odd_q[cut]
                        else:
                            direct, quad = even_d[cut] + odd_d[cut], even_q[cut] + odd_q[cut]
                        inverse = jnp.minimum(
                            lax.rsqrt(direct * direct + quad * quad), 1.0 / AMP_FLOOR
                        )
                        terms = (direct, direct * inverse, quad * inverse)
                        sums = [x + y for x, y in zip(sums, terms)]
                    for n, term in enumerate(sums):
                        acc[n, pl.ds(start, rows), at : at + COLS] += term
        return carry

    lax.fori_loop(0, pl.cdiv(total, BATCH // QUAD), add_batch, 0)

    pad = 128
    lags = 2 * bins
    span = lags + pad
    for g in range(NGRP):
        cut = slice(g * rows, (g + 1) * rows)
        root = jnp.sqrt(jnp.full((rows, lags), counts[g].astype(jnp.float32)))
        cosine, sine = acc[1, cut], acc[2, cut]
        coherence = jnp.sqrt(cosine * cosine + sine * sine) / root
        padded = jnp.concatenate([coherence, jnp.zeros((rows, pad), jnp.float32)], axis=1)
        part, smooth, at = padded, padded, 1
        for n in range(1, 5):
            part = part + pltpu.roll(part, span - (1 << (n - 1)), 1)
            smooth = smooth + pltpu.roll(part, span - at, 1)
            at += 1 << n
        smooth = pltpu.roll(smooth, HW, 1)[:, :lags] / (2 * HW + 1)
        out_ref[g] = ((acc[0, cut] / root) * smooth * smooth).astype(out_ref.dtype)


def whiten(values, order):
    bins = values.shape[1] // 2
    half = bins // 2
    values = values.astype(jnp.float32)
    power = jnp.sum(values * values, axis=-1, keepdims=True) * (1.0 / bins)
    whitened = (values / jnp.sqrt(power + EPSILON)).astype(jnp.bfloat16)
    real = jnp.dot(whitened[:, :bins], order, preferred_element_type=jnp.float32)
    imag = jnp.dot(whitened[:, bins:], order, preferred_element_type=jnp.float32)
    parts = (real[:, :half], imag[:, :half], real[:, half:], imag[:, half:])
    return [part.astype(jnp.bfloat16) for part in parts]


def whiten_kernel(spec_ref, out_ref):
    count, rows, width = spec_ref.shape
    half = width // 4
    parts = whiten(spec_ref[...].reshape(count * rows, width), bin_order(width // 2))
    for n, part in enumerate(parts):
        out_ref[:count, :, n * half : (n + 1) * half] = part.reshape(count, rows, half)
    out_ref[count] = jnp.zeros((rows, width), out_ref.dtype)


def greet(partners):
    barrier = pltpu.get_barrier_semaphore()
    for partner in partners:
        pl.semaphore_signal(
            barrier, inc=1, device_id=partner, device_id_type=pl.DeviceIdType.MESH
        )
    pl.semaphore_wait(barrier, len(partners))


def spread_kernel(
    size, lag_size, share, spec_ref, white_ref, held, order_ref, own_sem, send_sem, recv_sem,
):
    local_blocks, _, _, width = spec_ref.shape
    half = width // 4
    me = lax.axis_index("pair")
    lag = lax.axis_index("lag")

    chunk = local_blocks // CHUNKS if local_blocks % CHUNKS == 0 else local_blocks
    chunks = local_blocks // chunk

    def source(target, base, count):
        start = pl.multiple_of((target * lag_size + lag) * share, share)
        return spec_ref.at[base : base + count, 0, pl.ds(start, share), :]

    targets = [lax.rem(me + step, size) for step in range(1, size)]
    greet([{"pair": t} for t in targets])
    copies = {}
    for c in range(chunks):
        for n, target in enumerate(targets):
            copy = pltpu.make_async_remote_copy(
                src_ref=source(target, c * chunk, chunk),
                dst_ref=held.at[n + 1, c * chunk : (c + 1) * chunk],
                send_sem=send_sem.at[n * CHUNKS + c],
                recv_sem=recv_sem.at[n * CHUNKS + c],
                device_id={"pair": target},
                device_id_type=pl.DeviceIdType.MESH,
            )
            copy.start()
            copies[n + 1, c] = copy
    own = pltpu.make_async_copy(source(me, 0, local_blocks), held.at[0], own_sem)
    own.start()
    order_ref[...] = bin_order(width // 2)
    white_ref[local_blocks] = jnp.zeros(white_ref.shape[1:], white_ref.dtype)

    def finish(slot, base):
        origin = lax.rem(me - slot + size, size)
        values = held[slot, base : base + chunk].reshape(chunk * share, width)
        for n, part in enumerate(whiten(values, order_ref[...])):
            white_ref[base : base + chunk, origin, :, n * half : (n + 1) * half] = part.reshape(
                chunk, share, half
            )

    own.wait()
    for c in range(chunks):
        finish(0, c * chunk)
    for c in range(chunks):
        for step in sorted(range(1, size), key=lambda n: min(n, size - n)):
            copies[step, c].wait_recv()
            finish(step, c * chunk)
    for copy in copies.values():
        copy.wait_send()


def place_kernel(size, lag_size, share, piece, stack_ref, out_ref, own_sem, send_sem, recv_sem):
    me = lax.axis_index("pair") * lag_size + lax.axis_index("lag")
    rows = pl.ds(pl.multiple_of(me * share, share), share)

    def source(target):
        return stack_ref.at[:, :, pl.ds(pl.multiple_of(target * piece, piece), piece)]

    targets = [lax.rem(me + step, size) for step in range(1, size)]
    ids = [{"pair": lax.div(t, lag_size), "lag": lax.rem(t, lag_size)} for t in targets]
    greet(ids)
    copies = []
    for n, target in enumerate(targets):
        copy = pltpu.make_async_remote_copy(
            src_ref=source(target),
            dst_ref=out_ref.at[:, rows, :],
            send_sem=send_sem.at[n],
            recv_sem=recv_sem.at[n],
            device_id=ids[n],
            device_id_type=pl.DeviceIdType.MESH,
        )
        copy.start()
        copies.append(copy)
    own = pltpu.make_async_copy(source(me), out_ref.at[:, rows, :], own_sem)
    own.start()
    own.wait()
    for copy in copies:
        copy.wait()


def fused_kernel(
    size, lag_size, spec, pairs, live, groups, even_hbm, odd_hbm, out_ref,
    raw, send, whites, even_ref, odd_ref, order_ref, cross, prefix, stage, got,
    first_ids, second_ids, links, load_sem, table_sem, send_sem, recv_sem, give_sem, take_sem,
):
    local_blocks, _, _, width = spec.shape
    bins = width // 2
    half = bins // 2
    share = raw.shape[2]
    chunks = len(whites)
    devices = size * lag_size
    owners, slots = groups.shape
    quads = prefix.shape[1] - 1
    blank = whites[0].shape[0] - 1
    me = lax.axis_index("pair")
    lag = lax.axis_index("lag")
    place = me * lag_size + lag
    steps = [s for s in (2, 3, 1) if s < size] + [0]

    def device(step):
        return {
            "pair": lax.bitwise_xor(me, step // lag_size),
            "lag": lax.bitwise_xor(lag, step % lag_size),
        }

    barrier = pltpu.get_barrier_semaphore()
    for step in range(1, devices):
        pl.semaphore_signal(
            barrier, inc=1, device_id=device(step), device_id_type=pl.DeviceIdType.MESH
        )
    loads = []
    for n, step in enumerate(steps):
        target = lax.bitwise_xor(me, step)
        start = pl.multiple_of((target * lag_size + lag) * share, share)
        copy = pltpu.make_async_copy(
            spec.at[:, 0, pl.ds(start, share), :], raw.at[n], load_sem.at[n]
        )
        copy.start()
        loads.append(copy)
    fills = [
        pltpu.make_async_copy(even_hbm, even_ref, table_sem.at[0]),
        pltpu.make_async_copy(odd_hbm, odd_ref, table_sem.at[1]),
    ]
    for copy in fills:
        copy.start()
    order_ref[...] = bin_order(bins)

    low = lax.broadcasted_iota(jnp.int32, (local_blocks, 8, COLS), 1) < 4

    def swap(x):
        return pltpu.roll(x, 4, x.ndim - 2)

    def prepare(n):
        values = raw[n].reshape(local_blocks * share, width).astype(jnp.float32)
        power = jnp.sum(values * values, axis=-1, keepdims=True) * (1.0 / bins)
        whitened = (values * lax.rsqrt(power + EPSILON)).astype(jnp.bfloat16)
        for part in range(2):
            ordered = jnp.dot(
                whitened[:, part * bins : (part + 1) * bins], order_ref[...],
                preferred_element_type=jnp.float32,
            ).reshape(local_blocks, share, bins)
            for v in range(share // 8):
                tiles = [
                    ordered[:, 8 * v : 8 * v + 8, t * COLS : (t + 1) * COLS] for t in range(4)
                ]
                first = [jnp.where(low, tiles[2 * u], swap(tiles[2 * u + 1])) for u in range(2)]
                other = [jnp.where(low, swap(tiles[2 * u]), tiles[2 * u + 1]) for u in range(2)]
                for c, both in ((2 * v, first), (2 * v + 1, other)):
                    block = jnp.concatenate(both, axis=1).astype(jnp.bfloat16)
                    lanes = slice(part * COLS, (part + 1) * COLS)
                    if steps[n]:
                        send[c, n, :, :, lanes] = block
                    else:
                        whites[c][pl.ds(me * local_blocks, local_blocks), :, lanes] = block

    copies = {}

    def give(c, n):
        copy = pltpu.make_async_remote_copy(
            src_ref=send.at[c, n],
            dst_ref=whites[c].at[pl.ds(me * local_blocks, local_blocks)],
            send_sem=send_sem.at[c, n],
            recv_sem=recv_sem.at[c, n],
            device_id=device(steps[n] * lag_size),
            device_id_type=pl.DeviceIdType.MESH,
        )
        copy.start()
        copies[c, n] = copy

    for n in range(size):
        loads[n].wait()
        prepare(n)
        if n == 1:
            pl.semaphore_wait(barrier, devices - 1)
            give(0, 0)
            give(0, 1)
        if n == 2:
            give(0, 2)
            for c in range(1, chunks):
                for m in range(size - 1):
                    give(c, m)
    for white in whites:
        white[blank] = jnp.zeros(white.shape[1:], white.dtype)

    end = owners * slots

    def pick(g, values, default):
        for k in range(NGRP):
            default = jnp.where(g == k, values[k], default)
        return default

    def link_owner(p, carry):
        q = owners - 1 - p

        def link_slot(r, carry):
            heads, counts = carry
            s = slots - 1 - r
            g = groups[q, s]
            at = q * slots + s
            links[at] = pick(g, heads, end)
            used = s < live[q]
            hits = [jnp.logical_and(used, g == k) for k in range(NGRP)]
            heads = tuple(jnp.where(h, at, x) for h, x in zip(hits, heads))
            counts = tuple(jnp.where(h, x + 1, x) for h, x in zip(hits, counts))
            return heads, counts

        return lax.fori_loop(0, slots, link_slot, carry)

    zero = jnp.int32(0)
    last = jnp.int32(end)
    heads, counts = lax.fori_loop(0, owners, link_owner, ((last,) * NGRP, (zero,) * NGRP))
    links[end] = last

    def order_quad(n, carry):
        slot, group = carry
        for i in range(QUAD):
            stop = slot == end
            real = jnp.where(stop, 0, slot)
            q = real // slots
            s = real - q * slots

            def row(x):
                return jnp.where(stop, blank, (x % size) * local_blocks + x // size)

            first_ids[n * QUAD + i] = row(pairs[q, 0, s])
            second_ids[n * QUAD + i] = row(pairs[q, 1, s])
            slot = links[slot]
        done = slot == end
        group = jnp.where(done, group + 1, group)
        slot = jnp.where(done, pick(group, heads, last), slot)
        return slot, group

    lax.fori_loop(0, quads, order_quad, (heads[0], zero))
    ends = [zero]
    for k in range(NGRP):
        ends.append(ends[k] + (counts[k] + QUAD - 1) // QUAD)

    for n in range(3):
        prefix[n, 0] = jnp.zeros(prefix.shape[2:], prefix.dtype)
    for copy in fills:
        copy.wait()

    low8 = lax.broadcasted_iota(jnp.int32, (8, COLS), 0) < 4
    part_quads = quads // PARTS
    part_rows = part_quads * 16

    def fill_cross(white):
        def fill_quad(n, carry):
            products = []
            for i in range(QUAD):
                first = white[first_ids[n * QUAD + i]].astype(jnp.float32)
                second = white[second_ids[n * QUAD + i]].astype(jnp.float32)
                ra, ia = first[:, :COLS], first[:, COLS:]
                rb, ib = second[:, :COLS], second[:, COLS:]
                products.append((ra * rb + ia * ib, ia * rb - ra * ib))
            start = pl.multiple_of(n * 16, 16)
            for part in range(2):
                for h in range(2):
                    tops, bottoms = [], []
                    for i in range(0, QUAD, 2):
                        x = products[i][part][8 * h : 8 * h + 8]
                        y = products[i + 1][part][8 * h : 8 * h + 8]
                        tops.append(jnp.where(low8, x, swap(y)))
                        bottoms.append(jnp.where(low8, swap(x), y))
                    for j, tile in enumerate((tops, bottoms)):
                        at = (2 * part + j) * COLS
                        cross[h, pl.ds(start, 16), at : at + COLS] = jnp.concatenate(
                            tile, axis=0
                        ).astype(jnp.bfloat16)
            return carry

        lax.fori_loop(0, quads, fill_quad, 0)

    def add_part(p, carry):
        start = pl.multiple_of(p * part_rows, part_rows)
        base = p * part_quads
        for col in range(0, bins, COLS):
            def product(h, table):
                both = jnp.dot(
                    cross[h, pl.ds(start, part_rows), :],
                    table[:, 2 * col : 2 * (col + COLS)],
                    preferred_element_type=jnp.float32,
                )
                return both[:, :COLS], both[:, COLS:]

            even_d, even_q = product(0, even_ref)
            odd_d, odd_q = product(1, odd_ref)
            for side, at in ((-1, col), (1, bins + col)):
                sums = [prefix[n, base, :, at : at + COLS] for n in range(3)]
                for u in range(part_quads):
                    for i in range(2):
                        cut = slice(u * 16 + i * 8, u * 16 + i * 8 + 8)
                        if side < 0:
                            direct, quad = even_d[cut] - odd_d[cut], even_q[cut] - odd_q[cut]
                        else:
                            direct, quad = even_d[cut] + odd_d[cut], even_q[cut] + odd_q[cut]
                        inverse = jnp.minimum(
                            lax.rsqrt(direct * direct + quad * quad), 1.0 / AMP_FLOOR
                        )
                        terms = (direct, direct * inverse, quad * inverse)
                        sums = [x + y for x, y in zip(sums, terms)]
                    for n in range(3):
                        prefix[n, base + u + 1, :, at : at + COLS] = sums[n]
        return carry

    pad = 128
    lags = 2 * bins
    span = lags + pad
    piece = lags // devices
    low16 = lax.broadcasted_iota(jnp.int32, (8, lags), 0) < 4
    members = []
    for k in range(0, NGRP, 2):
        pair = [jnp.full((8, lags), counts[k + i].astype(jnp.float32)) for i in range(2)]
        members.append(jnp.where(low16, *pair))
    scale = 1.0 / jnp.sqrt(jnp.concatenate(members, axis=0))

    def stack(c):
        totals = []
        for n in range(3):
            rows = []
            for k in range(NGRP):
                total = prefix[n, ends[k + 1]] - prefix[n, ends[k]]
                rows.append(total + swap(total))
            totals.append(
                jnp.concatenate(
                    [jnp.where(low16, rows[k], rows[k + 1]) for k in range(0, NGRP, 2)], axis=0
                )
            )
        linear, cosine, sine = totals
        coherence = jnp.sqrt(cosine * cosine + sine * sine) * scale
        padded = jnp.concatenate([coherence, jnp.zeros((16, pad), jnp.float32)], axis=1)
        part, smooth, at = padded, padded, 1
        for n in range(1, 5):
            part = part + pltpu.roll(part, span - (1 << (n - 1)), 1)
            smooth = smooth + pltpu.roll(part, span - at, 1)
            at += 1 << n
        smooth = pltpu.roll(smooth, HW, 1)[:, :lags] * (1.0 / (2 * HW + 1))
        result = (linear * scale * smooth * smooth).astype(jnp.bfloat16)
        for t in range(devices):
            stage[c, t] = result[:, t * piece : (t + 1) * piece]
        got[c, place] = stage[c, place]
        for step in range(1, devices):
            target = device(step)
            copy = pltpu.make_async_remote_copy(
                src_ref=stage.at[c, target["pair"] * lag_size + target["lag"]],
                dst_ref=got.at[c, place],
                send_sem=give_sem.at[c, step - 1],
                recv_sem=take_sem.at[c, step - 1],
                device_id=target,
                device_id_type=pl.DeviceIdType.MESH,
            )
            copy.start()
            results[c, step] = copy

    low_out = lax.broadcasted_iota(jnp.int32, (devices, 8, piece), 1) < 4

    def assemble(v):
        for c in (2 * v, 2 * v + 1):
            for step in range(1, devices):
                results[c, step].wait_recv()
        a = got[2 * v].astype(jnp.float32)
        b = got[2 * v + 1].astype(jnp.float32)
        for k in range(0, NGRP, 2):
            x, y = a[:, 4 * k : 4 * k + 8], b[:, 4 * k : 4 * k + 8]
            out_ref[k, :, 8 * v : 8 * v + 8, :] = jnp.where(low_out, x, swap(y))
            out_ref[k + 1, :, 8 * v : 8 * v + 8, :] = jnp.where(low_out, swap(x), y)

    results = {}
    for c in range(chunks):
        for n in range(size - 1):
            copies[c, n].wait_recv()
        fill_cross(whites[c])
        lax.fori_loop(0, PARTS, add_part, 0)
        stack(c)
        if c >= 2 and c % 2 == 0:
            assemble(c // 2 - 1)
    assemble(chunks // 2 - 1)
    for copy in copies.values():
        copy.wait_send()
    for copy in results.values():
        copy.wait_send()


def fused(spectra, pairs, live, groups, even, odd, pair_size, lag_size, share):
    local_blocks, _, _, width = spectra.shape
    owners, slots = groups.shape
    blocks = local_blocks * pair_size
    devices = pair_size * lag_size
    chunks = share // CHUNK_ROWS
    quads = -(-(owners * slots // QUAD + NGRP) // PARTS) * PARTS
    piece = width // devices
    smem = pl.BlockSpec(memory_space=pltpu.SMEM)
    hbm = pl.BlockSpec(memory_space=pltpu.HBM)
    dma = pltpu.SemaphoreType.DMA
    out = pl.pallas_call(
        functools.partial(fused_kernel, pair_size, lag_size),
        out_shape=jax.ShapeDtypeStruct((NGRP, devices, share, piece), jnp.float32),
        in_specs=[hbm] + [smem] * 3 + [hbm] * 2,
        out_specs=pl.BlockSpec(memory_space=pltpu.VMEM),
        scratch_shapes=[
            pltpu.VMEM((pair_size, local_blocks, share, width), jnp.bfloat16),
            pltpu.VMEM((chunks, pair_size - 1, local_blocks, 16, 2 * COLS), jnp.bfloat16),
            [pltpu.VMEM((blocks + 1, 16, 2 * COLS), jnp.bfloat16)] * chunks,
            pltpu.VMEM(even.shape, jnp.bfloat16),
            pltpu.VMEM(odd.shape, jnp.bfloat16),
            pltpu.VMEM((width // 2, width // 2), jnp.bfloat16),
            pltpu.VMEM((2, quads * 16, width // 2), jnp.bfloat16),
            pltpu.VMEM((3, quads + 1, 8, width), jnp.float32),
            pltpu.VMEM((chunks, devices, 16, piece), jnp.bfloat16),
            pltpu.VMEM((chunks, devices, 16, piece), jnp.bfloat16),
            pltpu.SMEM((quads * QUAD,), jnp.int32),
            pltpu.SMEM((quads * QUAD,), jnp.int32),
            pltpu.SMEM((owners * slots + 1,), jnp.int32),
            dma((pair_size,)),
            dma((2,)),
            dma((chunks, pair_size - 1)),
            dma((chunks, pair_size - 1)),
            dma((chunks, devices - 1)),
            dma((chunks, devices - 1)),
        ],
        compiler_params=pltpu.CompilerParams(
            collective_id=2, has_side_effects=True, vmem_limit_bytes=50 << 20
        ),
    )(spectra, pairs, live, groups, even, odd)
    return out.reshape(NGRP, devices * share, piece)


def semaphores(count):
    return [
        pltpu.SemaphoreType.DMA,
        pltpu.SemaphoreType.DMA((count,)),
        pltpu.SemaphoreType.DMA((count,)),
    ]


def spread(spectra, pair_size, lag_size, share):
    local_blocks, _, _, width = spectra.shape
    blocks = local_blocks * pair_size
    vmem = pl.BlockSpec(memory_space=pltpu.VMEM)
    params = dict(vmem_limit_bytes=50 << 20)
    if share % ROWS:
        cells = spectra.reshape(local_blocks, pair_size, lag_size, share, width)
        cells = lax.dynamic_index_in_dim(cells, lax.axis_index("lag"), 2, keepdims=False)
        moved = lax.all_to_all(cells, "pair", 1, 1, tiled=True).reshape(blocks, share, width)
        rows = -(-share // ROWS) * ROWS
        return pl.pallas_call(
            whiten_kernel,
            out_shape=jax.ShapeDtypeStruct((blocks + 1, rows, width), jnp.bfloat16),
            in_specs=[vmem],
            out_specs=vmem,
            compiler_params=pltpu.CompilerParams(**params),
        )(jnp.pad(moved, ((0, 0), (0, rows - share), (0, 0))))
    white = pl.pallas_call(
        functools.partial(spread_kernel, pair_size, lag_size, share),
        out_shape=jax.ShapeDtypeStruct((local_blocks + 1, pair_size, share, width), jnp.bfloat16),
        in_specs=[pl.BlockSpec(memory_space=pltpu.HBM)],
        out_specs=vmem,
        scratch_shapes=[
            pltpu.VMEM((pair_size, local_blocks, share, width), spectra.dtype),
            pltpu.VMEM((width // 2, width // 2), jnp.bfloat16),
        ]
        + semaphores((pair_size - 1) * CHUNKS),
        compiler_params=pltpu.CompilerParams(collective_id=0, has_side_effects=True, **params),
    )(spectra)
    return white.reshape(blocks + pair_size, share, width)


def place(stacks, pair_size, lag_size, share):
    size = pair_size * lag_size
    groups, _, lags = stacks.shape
    piece = lags // size
    if share % ROWS or piece % 128:
        return lax.all_to_all(stacks[:, :share], ("pair", "lag"), 2, 1, tiled=True)
    return pl.pallas_call(
        functools.partial(place_kernel, size, lag_size, share, piece),
        out_shape=jax.ShapeDtypeStruct((groups, size * share, piece), stacks.dtype),
        in_specs=[pl.BlockSpec(memory_space=pl.ANY)],
        out_specs=pl.BlockSpec(memory_space=pltpu.VMEM),
        scratch_shapes=semaphores(size - 1),
        compiler_params=pltpu.CompilerParams(collective_id=1, has_side_effects=True),
    )(stacks)


def shards(spectra, pair_blocks, live_pairs, stack_group):
    pair_size = lax.axis_size("pair")
    lag_size = lax.axis_size("lag")
    _, _, channels, width = spectra.shape
    share = channels // (pair_size * lag_size)
    owners, slots = stack_group.shape
    even, odd = tables(width // 2)
    if share == ROWS and width == 8 * COLS and pair_size == 4 and lag_size == 2:
        pairs = pair_blocks.transpose(0, 2, 1)
        return fused(
            spectra, pairs, live_pairs, stack_group, even, odd, pair_size, lag_size, share
        )
    white = spread(spectra, pair_size, lag_size, share)
    rows = white.shape[1]
    smem = pl.BlockSpec(memory_space=pltpu.SMEM)
    vmem = pl.BlockSpec(memory_space=pltpu.VMEM)
    ids = pltpu.SMEM((NGRP * (owners * slots + QUAD) + QUAD,), jnp.int32)
    quads = pltpu.SMEM((owners * slots // QUAD + NGRP + BATCH,), jnp.int32)
    stacks = pl.pallas_call(
        kernel,
        out_shape=jax.ShapeDtypeStruct((NGRP, rows, width), jnp.bfloat16),
        in_specs=[smem] * 3 + [vmem] * 3,
        out_specs=vmem,
        scratch_shapes=[
            pltpu.VMEM((BATCH * rows, width), jnp.bfloat16),
            pltpu.VMEM((3, NGRP * rows, width), jnp.float32),
            ids, ids, quads, quads,
            pltpu.SMEM((NGRP,), jnp.int32),
        ],
        compiler_params=pltpu.CompilerParams(vmem_limit_bytes=40 << 20),
    )(
        pair_blocks.transpose(0, 2, 1), live_pairs, stack_group, white, even, odd
    )
    return place(stacks, pair_size, lag_size, share).astype(jnp.float32)


def solution(mesh):
    return jax.shard_map(
        shards,
        mesh=mesh,
        in_specs=(P("win", "pair", "stk", None), P("win", None, None), P("win"), P("win", None)),
        out_specs=P("win", "stk", ("pair", "lag")),
        check_vma=False,
    )
```

```python
import functools
import math

import jax
import jax.numpy as jnp
import numpy as np
from jax import lax
from jax.experimental import pallas as pl
from jax.experimental.pallas import tpu as pltpu
from jax.sharding import PartitionSpec as P

NGRP = 4
HW = 15
AMP_FLOOR = 0.5
EPSILON = 1e-06
ROWS = 16
BATCH = 16
QUAD = 4
CHUNKS = 4
COLS = 128
CHUNK_ROWS = 4
PARTS = 2


def tables(num_bins):
    bins = np.arange(num_bins)[:, None]
    steps = np.arange(num_bins)[None, :]
    angles = (bins * steps % (2 * num_bins)) * (math.pi / num_bins)
    scale = math.sqrt(2.0 / num_bins)
    cosine = np.cos(angles) * scale
    sine = np.sin(angles) * scale
    upper = np.concatenate([cosine, sine], axis=1)
    lower = np.concatenate([-sine, cosine], axis=1)
    even = np.concatenate([upper[0::2], lower[0::2]], axis=0)
    odd = np.concatenate([upper[1::2], lower[1::2]], axis=0)
    shape = (num_bins, 2, num_bins // COLS, COLS)
    even, odd = (t.reshape(shape).swapaxes(1, 2).reshape(t.shape) for t in (even, odd))
    return tuple(jnp.asarray(t, jnp.bfloat16) for t in (even, odd))


def bin_order(bins):
    row = lax.broadcasted_iota(jnp.int32, (bins, bins), 0)
    col = lax.broadcasted_iota(jnp.int32, (bins, bins), 1)
    place = jnp.where(col < bins // 2, 2 * col, 2 * col - (bins - 1))
    return jnp.where(row == place, 1.0, 0.0).astype(jnp.bfloat16)


def kernel(
    pairs, live, groups, white, even_ref, odd_ref, out_ref,
    cross, acc, first_ids, second_ids, quad_at, quad_group, counts,
):
    owners = live.shape[0]
    blocks, (_, rows, width) = white.shape[0] - 1, white.shape
    bins = width // 2
    half = bins // 2

    stride = (first_ids.shape[0] - QUAD) // NGRP

    def add_owner(q, carry):
        def add_slot(s, carry):
            group = groups[q, s]
            count = counts[group]
            at = group * stride + count
            first_ids[at] = pairs[q, 0, s]
            second_ids[at] = pairs[q, 1, s]
            counts[group] = count + 1
            return carry

        return lax.fori_loop(0, live[q], add_slot, carry)

    for g in range(NGRP):
        counts[g] = 0
    lax.fori_loop(0, owners, add_owner, 0)

    def blank(at):
        for i in range(QUAD):
            first_ids[at + i] = blocks
            second_ids[at + i] = blocks

    total = 0
    for g in range(NGRP):
        blank(g * stride + counts[g])

        def add_quad(n, total, g=g):
            quad_at[total] = g * stride + n * QUAD
            quad_group[total] = g
            return total + 1

        total = lax.fori_loop(0, pl.cdiv(counts[g], QUAD), add_quad, total)
    blank(NGRP * stride)
    for i in range(BATCH // QUAD):
        quad_at[total + i] = NGRP * stride
        quad_group[total + i] = 0

    acc[...] = jnp.zeros_like(acc)

    def add_batch(step, carry):
        base = step * (BATCH // QUAD)
        for i in range(BATCH):
            at = quad_at[base + i // QUAD] + i % QUAD
            first = white[first_ids[at]].astype(jnp.float32)
            second = white[second_ids[at]].astype(jnp.float32)
            for n in range(2):
                lo, mid, hi = 2 * n * half, (2 * n + 1) * half, (2 * n + 2) * half
                ra, ia = first[:, lo:mid], first[:, mid:hi]
                rb, ib = second[:, lo:mid], second[:, mid:hi]
                cross[i * rows : (i + 1) * rows, lo:mid] = (ra * rb + ia * ib).astype(jnp.bfloat16)
                cross[i * rows : (i + 1) * rows, mid:hi] = (ia * rb - ra * ib).astype(jnp.bfloat16)
        for col in range(0, bins, COLS):
            def product(n, table):
                both = jnp.dot(
                    cross[:, n * bins : (n + 1) * bins],
                    table[:, 2 * col : 2 * (col + COLS)],
                    preferred_element_type=jnp.float32,
                )
                return both[:, :COLS], both[:, COLS:]

            even_d, even_q = product(0, even_ref)
            odd_d, odd_q = product(1, odd_ref)
            for u in range(BATCH // QUAD):
                start = pl.multiple_of(quad_group[base + u] * rows, rows)
                for side, at in ((-1, col), (1, bins + col)):
                    sums = [0.0, 0.0, 0.0]
                    for i in range(u * QUAD, (u + 1) * QUAD):
                        cut = slice(i * rows, (i + 1) * rows)
                        if side < 0:
                            direct, quad = even_d[cut] - odd_d[cut], even_q[cut] - odd_q[cut]
                        else:
                            direct, quad = even_d[cut] + odd_d[cut], even_q[cut] + odd_q[cut]
                        inverse = jnp.minimum(
                            lax.rsqrt(direct * direct + quad * quad), 1.0 / AMP_FLOOR
                        )
                        terms = (direct, direct * inverse, quad * inverse)
                        sums = [x + y for x, y in zip(sums, terms)]
                    for n, term in enumerate(sums):
                        acc[n, pl.ds(start, rows), at : at + COLS] += term
        return carry

    lax.fori_loop(0, pl.cdiv(total, BATCH // QUAD), add_batch, 0)

    pad = 128
    lags = 2 * bins
    span = lags + pad
    for g in range(NGRP):
        cut = slice(g * rows, (g + 1) * rows)
        root = jnp.sqrt(jnp.full((rows, lags), counts[g].astype(jnp.float32)))
        cosine, sine = acc[1, cut], acc[2, cut]
        coherence = jnp.sqrt(cosine * cosine + sine * sine) / root
        padded = jnp.concatenate([coherence, jnp.zeros((rows, pad), jnp.float32)], axis=1)
        part, smooth, at = padded, padded, 1
        for n in range(1, 5):
            part = part + pltpu.roll(part, span - (1 << (n - 1)), 1)
            smooth = smooth + pltpu.roll(part, span - at, 1)
            at += 1 << n
        smooth = pltpu.roll(smooth, HW, 1)[:, :lags] / (2 * HW + 1)
        out_ref[g] = ((acc[0, cut] / root) * smooth * smooth).astype(out_ref.dtype)


def whiten(values, order):
    bins = values.shape[1] // 2
    half = bins // 2
    values = values.astype(jnp.float32)
    power = jnp.sum(values * values, axis=-1, keepdims=True) * (1.0 / bins)
    whitened = (values / jnp.sqrt(power + EPSILON)).astype(jnp.bfloat16)
    real = jnp.dot(whitened[:, :bins], order, preferred_element_type=jnp.float32)
    imag = jnp.dot(whitened[:, bins:], order, preferred_element_type=jnp.float32)
    parts = (real[:, :half], imag[:, :half], real[:, half:], imag[:, half:])
    return [part.astype(jnp.bfloat16) for part in parts]


def whiten_kernel(spec_ref, out_ref):
    count, rows, width = spec_ref.shape
    half = width // 4
    parts = whiten(spec_ref[...].reshape(count * rows, width), bin_order(width // 2))
    for n, part in enumerate(parts):
        out_ref[:count, :, n * half : (n + 1) * half] = part.reshape(count, rows, half)
    out_ref[count] = jnp.zeros((rows, width), out_ref.dtype)


def greet(partners):
    barrier = pltpu.get_barrier_semaphore()
    for partner in partners:
        pl.semaphore_signal(
            barrier, inc=1, device_id=partner, device_id_type=pl.DeviceIdType.MESH
        )
    pl.semaphore_wait(barrier, len(partners))


def spread_kernel(
    size, lag_size, share, spec_ref, white_ref, held, order_ref, own_sem, send_sem, recv_sem,
):
    local_blocks, _, _, width = spec_ref.shape
    half = width // 4
    me = lax.axis_index("pair")
    lag = lax.axis_index("lag")

    chunk = local_blocks // CHUNKS if local_blocks % CHUNKS == 0 else local_blocks
    chunks = local_blocks // chunk

    def source(target, base, count):
        start = pl.multiple_of((target * lag_size + lag) * share, share)
        return spec_ref.at[base : base + count, 0, pl.ds(start, share), :]

    targets = [lax.rem(me + step, size) for step in range(1, size)]
    greet([{"pair": t} for t in targets])
    copies = {}
    for c in range(chunks):
        for n, target in enumerate(targets):
            copy = pltpu.make_async_remote_copy(
                src_ref=source(target, c * chunk, chunk),
                dst_ref=held.at[n + 1, c * chunk : (c + 1) * chunk],
                send_sem=send_sem.at[n * CHUNKS + c],
                recv_sem=recv_sem.at[n * CHUNKS + c],
                device_id={"pair": target},
                device_id_type=pl.DeviceIdType.MESH,
            )
            copy.start()
            copies[n + 1, c] = copy
    own = pltpu.make_async_copy(source(me, 0, local_blocks), held.at[0], own_sem)
    own.start()
    order_ref[...] = bin_order(width // 2)
    white_ref[local_blocks] = jnp.zeros(white_ref.shape[1:], white_ref.dtype)

    def finish(slot, base):
        origin = lax.rem(me - slot + size, size)
        values = held[slot, base : base + chunk].reshape(chunk * share, width)
        for n, part in enumerate(whiten(values, order_ref[...])):
            white_ref[base : base + chunk, origin, :, n * half : (n + 1) * half] = part.reshape(
                chunk, share, half
            )

    own.wait()
    for c in range(chunks):
        finish(0, c * chunk)
    for c in range(chunks):
        for step in sorted(range(1, size), key=lambda n: min(n, size - n)):
            copies[step, c].wait_recv()
            finish(step, c * chunk)
    for copy in copies.values():
        copy.wait_send()


def place_kernel(size, lag_size, share, piece, stack_ref, out_ref, own_sem, send_sem, recv_sem):
    me = lax.axis_index("pair") * lag_size + lax.axis_index("lag")
    rows = pl.ds(pl.multiple_of(me * share, share), share)

    def source(target):
        return stack_ref.at[:, :, pl.ds(pl.multiple_of(target * piece, piece), piece)]

    targets = [lax.rem(me + step, size) for step in range(1, size)]
    ids = [{"pair": lax.div(t, lag_size), "lag": lax.rem(t, lag_size)} for t in targets]
    greet(ids)
    copies = []
    for n, target in enumerate(targets):
        copy = pltpu.make_async_remote_copy(
            src_ref=source(target),
            dst_ref=out_ref.at[:, rows, :],
            send_sem=send_sem.at[n],
            recv_sem=recv_sem.at[n],
            device_id=ids[n],
            device_id_type=pl.DeviceIdType.MESH,
        )
        copy.start()
        copies.append(copy)
    own = pltpu.make_async_copy(source(me), out_ref.at[:, rows, :], own_sem)
    own.start()
    own.wait()
    for copy in copies:
        copy.wait()


def fused_kernel(
    size, lag_size, spec, pairs_hbm, live_hbm, groups_hbm, even_hbm, odd_hbm, out_ref,
    raw, send, whites, even_ref, odd_ref, order_ref, cross, prefix, stage, got,
    pairs, live, groups, first_ids, second_ids, links, load_sem, table_sem, send_sem, recv_sem, give_sem, take_sem,
):
    local_blocks, _, _, width = spec.shape
    bins = width // 2
    half = bins // 2
    share = raw.shape[2]
    chunks = len(whites)
    devices = size * lag_size
    owners, slots = groups.shape
    quads = prefix.shape[1] - 1
    blank = whites[0].shape[0] - 1
    me = lax.axis_index("pair")
    lag = lax.axis_index("lag")
    place = me * lag_size + lag
    steps = [s for s in (2, 3, 1) if s < size] + [0]

    def device(step):
        return {
            "pair": lax.bitwise_xor(me, step // lag_size),
            "lag": lax.bitwise_xor(lag, step % lag_size),
        }

    barrier = pltpu.get_barrier_semaphore()
    for step in range(1, devices):
        pl.semaphore_signal(
            barrier, inc=1, device_id=device(step), device_id_type=pl.DeviceIdType.MESH
        )
    loads = []
    for n, step in enumerate(steps):
        target = lax.bitwise_xor(me, step)
        start = pl.multiple_of((target * lag_size + lag) * share, share)
        copy = pltpu.make_async_copy(
            spec.at[:, 0, pl.ds(start, share), :], raw.at[n], load_sem.at[n]
        )
        copy.start()
        loads.append(copy)
    fills = [
        pltpu.make_async_copy(even_hbm, even_ref, table_sem.at[0]),
        pltpu.make_async_copy(odd_hbm, odd_ref, table_sem.at[1]),
    ]
    plans = [
        pltpu.make_async_copy(pairs_hbm, pairs, table_sem.at[2]),
        pltpu.make_async_copy(live_hbm, live, table_sem.at[3]),
        pltpu.make_async_copy(groups_hbm, groups, table_sem.at[4]),
    ]
    for copy in plans + fills:
        copy.start()
    order_ref[...] = bin_order(bins)

    low = lax.broadcasted_iota(jnp.int32, (local_blocks, 8, COLS), 1) < 4

    def swap(x):
        return pltpu.roll(x, 4, x.ndim - 2)

    def prepare(n):
        values = raw[n].reshape(local_blocks * share, width).astype(jnp.float32)
        power = jnp.sum(values * values, axis=-1, keepdims=True) * (1.0 / bins)
        whitened = (values * lax.rsqrt(power + EPSILON)).astype(jnp.bfloat16)
        for part in range(2):
            ordered = jnp.dot(
                whitened[:, part * bins : (part + 1) * bins], order_ref[...],
                preferred_element_type=jnp.float32,
            ).reshape(local_blocks, share, bins)
            for v in range(share // 8):
                tiles = [
                    ordered[:, 8 * v : 8 * v + 8, t * COLS : (t + 1) * COLS] for t in range(4)
                ]
                first = [jnp.where(low, tiles[2 * u], swap(tiles[2 * u + 1])) for u in range(2)]
                other = [jnp.where(low, swap(tiles[2 * u]), tiles[2 * u + 1]) for u in range(2)]
                for c, both in ((2 * v, first), (2 * v + 1, other)):
                    block = jnp.concatenate(both, axis=1).astype(jnp.bfloat16)
                    lanes = slice(part * COLS, (part + 1) * COLS)
                    if steps[n]:
                        send[c, n, :, :, lanes] = block
                    else:
                        whites[c][pl.ds(me * local_blocks, local_blocks), :, lanes] = block

    copies = {}

    def give(c, n):
        copy = pltpu.make_async_remote_copy(
            src_ref=send.at[c, n],
            dst_ref=whites[c].at[pl.ds(me * local_blocks, local_blocks)],
            send_sem=send_sem.at[c, n],
            recv_sem=recv_sem.at[c, n],
            device_id=device(steps[n] * lag_size),
            device_id_type=pl.DeviceIdType.MESH,
        )
        copy.start()
        copies[c, n] = copy

    for n in range(size):
        loads[n].wait()
        prepare(n)
        if n == 1:
            pl.semaphore_wait(barrier, devices - 1)
            give(0, 0)
            give(0, 1)
        if n == 2:
            give(0, 2)
            for c in range(1, chunks):
                for m in range(size - 1):
                    give(c, m)
    for white in whites:
        white[blank] = jnp.zeros(white.shape[1:], white.dtype)

    end = owners * slots
    for copy in plans:
        copy.wait()

    def pick(g, values, default):
        for k in range(NGRP):
            default = jnp.where(g == k, values[k], default)
        return default

    def link_owner(p, carry):
        q = owners - 1 - p

        def link_slot(r, carry):
            heads, counts = carry
            s = slots - 1 - r
            g = groups[q, s]
            at = q * slots + s
            links[at] = pick(g, heads, end)
            used = s < live[q]
            hits = [jnp.logical_and(used, g == k) for k in range(NGRP)]
            heads = tuple(jnp.where(h, at, x) for h, x in zip(hits, heads))
            counts = tuple(jnp.where(h, x + 1, x) for h, x in zip(hits, counts))
            return heads, counts

        return lax.fori_loop(0, slots, link_slot, carry)

    zero = jnp.int32(0)
    last = jnp.int32(end)
    heads, counts = lax.fori_loop(0, owners, link_owner, ((last,) * NGRP, (zero,) * NGRP))
    links[end] = last

    def order_quad(n, carry):
        slot, group = carry
        for i in range(QUAD):
            stop = slot == end
            real = jnp.where(stop, 0, slot)
            q = real // slots
            s = real - q * slots

            def row(x):
                return jnp.where(stop, blank, (x % size) * local_blocks + x // size)

            first_ids[n * QUAD + i] = row(pairs[q, 0, s])
            second_ids[n * QUAD + i] = row(pairs[q, 1, s])
            slot = links[slot]
        done = slot == end
        group = jnp.where(done, group + 1, group)
        slot = jnp.where(done, pick(group, heads, last), slot)
        return slot, group

    lax.fori_loop(0, quads, order_quad, (heads[0], zero))
    ends = [zero]
    for k in range(NGRP):
        ends.append(ends[k] + (counts[k] + QUAD - 1) // QUAD)

    for n in range(3):
        prefix[n, 0] = jnp.zeros(prefix.shape[2:], prefix.dtype)
    for copy in fills:
        copy.wait()

    low8 = lax.broadcasted_iota(jnp.int32, (8, COLS), 0) < 4
    part_quads = quads // PARTS
    part_rows = part_quads * 16

    def fill_cross(white):
        def fill_quad(n, carry):
            products = []
            for i in range(QUAD):
                first = white[first_ids[n * QUAD + i]].astype(jnp.float32)
                second = white[second_ids[n * QUAD + i]].astype(jnp.float32)
                ra, ia = first[:, :COLS], first[:, COLS:]
                rb, ib = second[:, :COLS], second[:, COLS:]
                products.append((ra * rb + ia * ib, ia * rb - ra * ib))
            start = pl.multiple_of(n * 16, 16)
            for part in range(2):
                for h in range(2):
                    tops, bottoms = [], []
                    for i in range(0, QUAD, 2):
                        x = products[i][part][8 * h : 8 * h + 8]
                        y = products[i + 1][part][8 * h : 8 * h + 8]
                        tops.append(jnp.where(low8, x, swap(y)))
                        bottoms.append(jnp.where(low8, swap(x), y))
                    for j, tile in enumerate((tops, bottoms)):
                        at = (2 * part + j) * COLS
                        cross[h, pl.ds(start, 16), at : at + COLS] = jnp.concatenate(
                            tile, axis=0
                        ).astype(jnp.bfloat16)
            return carry

        lax.fori_loop(0, quads, fill_quad, 0)

    def add_part(p, carry):
        start = pl.multiple_of(p * part_rows, part_rows)
        base = p * part_quads
        for col in range(0, bins, COLS):
            def product(h, table):
                both = jnp.dot(
                    cross[h, pl.ds(start, part_rows), :],
                    table[:, 2 * col : 2 * (col + COLS)],
                    preferred_element_type=jnp.float32,
                )
                return both[:, :COLS], both[:, COLS:]

            even_d, even_q = product(0, even_ref)
            odd_d, odd_q = product(1, odd_ref)
            for side, at in ((-1, col), (1, bins + col)):
                sums = [prefix[n, base, :, at : at + COLS] for n in range(3)]
                for u in range(part_quads):
                    for i in range(2):
                        cut = slice(u * 16 + i * 8, u * 16 + i * 8 + 8)
                        if side < 0:
                            direct, quad = even_d[cut] - odd_d[cut], even_q[cut] - odd_q[cut]
                        else:
                            direct, quad = even_d[cut] + odd_d[cut], even_q[cut] + odd_q[cut]
                        inverse = jnp.minimum(
                            lax.rsqrt(direct * direct + quad * quad), 1.0 / AMP_FLOOR
                        )
                        terms = (direct, direct * inverse, quad * inverse)
                        sums = [x + y for x, y in zip(sums, terms)]
                    for n in range(3):
                        prefix[n, base + u + 1, :, at : at + COLS] = sums[n]
        return carry

    pad = 128
    lags = 2 * bins
    span = lags + pad
    piece = lags // devices
    low16 = lax.broadcasted_iota(jnp.int32, (8, lags), 0) < 4
    members = []
    for k in range(0, NGRP, 2):
        pair = [jnp.full((8, lags), counts[k + i].astype(jnp.float32)) for i in range(2)]
        members.append(jnp.where(low16, *pair))
    scale = 1.0 / jnp.sqrt(jnp.concatenate(members, axis=0))

    def stack(c):
        totals = []
        for n in range(3):
            rows = []
            for k in range(NGRP):
                total = prefix[n, ends[k + 1]] - prefix[n, ends[k]]
                rows.append(total + swap(total))
            totals.append(
                jnp.concatenate(
                    [jnp.where(low16, rows[k], rows[k + 1]) for k in range(0, NGRP, 2)], axis=0
                )
            )
        linear, cosine, sine = totals
        coherence = jnp.sqrt(cosine * cosine + sine * sine) * scale
        padded = jnp.concatenate([coherence, jnp.zeros((16, pad), jnp.float32)], axis=1)
        part, smooth, at = padded, padded, 1
        for n in range(1, 5):
            part = part + pltpu.roll(part, span - (1 << (n - 1)), 1)
            smooth = smooth + pltpu.roll(part, span - at, 1)
            at += 1 << n
        smooth = pltpu.roll(smooth, HW, 1)[:, :lags] * (1.0 / (2 * HW + 1))
        result = (linear * scale * smooth * smooth).astype(jnp.bfloat16)
        for t in range(devices):
            stage[c, t] = result[:, t * piece : (t + 1) * piece]
        got[c, place] = stage[c, place]
        for step in range(1, devices):
            target = device(step)
            copy = pltpu.make_async_remote_copy(
                src_ref=stage.at[c, target["pair"] * lag_size + target["lag"]],
                dst_ref=got.at[c, place],
                send_sem=give_sem.at[c, step - 1],
                recv_sem=take_sem.at[c, step - 1],
                device_id=target,
                device_id_type=pl.DeviceIdType.MESH,
            )
            copy.start()
            results[c, step] = copy

    low_out = lax.broadcasted_iota(jnp.int32, (devices, 8, piece), 1) < 4

    def assemble(v):
        for c in (2 * v, 2 * v + 1):
            for step in range(1, devices):
                results[c, step].wait_recv()
        a = got[2 * v].astype(jnp.float32)
        b = got[2 * v + 1].astype(jnp.float32)
        for k in range(0, NGRP, 2):
            x, y = a[:, 4 * k : 4 * k + 8], b[:, 4 * k : 4 * k + 8]
            out_ref[k, :, 8 * v : 8 * v + 8, :] = jnp.where(low_out, x, swap(y))
            out_ref[k + 1, :, 8 * v : 8 * v + 8, :] = jnp.where(low_out, swap(x), y)

    results = {}
    for c in range(chunks):
        for n in range(size - 1):
            copies[c, n].wait_recv()
        fill_cross(whites[c])
        lax.fori_loop(0, PARTS, add_part, 0)
        stack(c)
        if c >= 2 and c % 2 == 0:
            assemble(c // 2 - 1)
    assemble(chunks // 2 - 1)
    for copy in copies.values():
        copy.wait_send()
    for copy in results.values():
        copy.wait_send()


def fused(spectra, pairs, live, groups, even, odd, pair_size, lag_size, share):
    local_blocks, _, _, width = spectra.shape
    owners, slots = groups.shape
    blocks = local_blocks * pair_size
    devices = pair_size * lag_size
    chunks = share // CHUNK_ROWS
    quads = -(-(owners * slots // QUAD + NGRP) // PARTS) * PARTS
    piece = width // devices
    operands = (spectra, pairs, live, groups, even, odd)
    hbm = pl.BlockSpec(memory_space=pltpu.HBM)
    dma = pltpu.SemaphoreType.DMA
    out = pl.pallas_call(
        functools.partial(fused_kernel, pair_size, lag_size),
        out_shape=jax.ShapeDtypeStruct((NGRP, devices, share, piece), jnp.float32),
        in_specs=[hbm] * 6,
        out_specs=pl.BlockSpec(memory_space=pltpu.VMEM),
        scratch_shapes=[
            pltpu.VMEM((pair_size, local_blocks, share, width), jnp.bfloat16),
            pltpu.VMEM((chunks, pair_size - 1, local_blocks, 16, 2 * COLS), jnp.bfloat16),
            [pltpu.VMEM((blocks + 1, 16, 2 * COLS), jnp.bfloat16)] * chunks,
            pltpu.VMEM(even.shape, jnp.bfloat16),
            pltpu.VMEM(odd.shape, jnp.bfloat16),
            pltpu.VMEM((width // 2, width // 2), jnp.bfloat16),
            pltpu.VMEM((2, quads * 16, width // 2), jnp.bfloat16),
            pltpu.VMEM((3, quads + 1, 8, width), jnp.float32),
            pltpu.VMEM((chunks, devices, 16, piece), jnp.bfloat16),
            pltpu.VMEM((chunks, devices, 16, piece), jnp.bfloat16),
            pltpu.SMEM(pairs.shape, jnp.int32),
            pltpu.SMEM(live.shape, jnp.int32),
            pltpu.SMEM(groups.shape, jnp.int32),
            pltpu.SMEM((quads * QUAD,), jnp.int32),
            pltpu.SMEM((quads * QUAD,), jnp.int32),
            pltpu.SMEM((owners * slots + 1,), jnp.int32),
            dma((pair_size,)),
            dma((5,)),
            dma((chunks, pair_size - 1)),
            dma((chunks, pair_size - 1)),
            dma((chunks, devices - 1)),
            dma((chunks, devices - 1)),
        ],
        compiler_params=pltpu.CompilerParams(
            collective_id=2, has_side_effects=True, vmem_limit_bytes=50 << 20
        ),
    )(*(pltpu.with_memory_space_constraint(x, pltpu.HBM) for x in operands))
    return out.reshape(NGRP, devices * share, piece)


def semaphores(count):
    return [
        pltpu.SemaphoreType.DMA,
        pltpu.SemaphoreType.DMA((count,)),
        pltpu.SemaphoreType.DMA((count,)),
    ]


def spread(spectra, pair_size, lag_size, share):
    local_blocks, _, _, width = spectra.shape
    blocks = local_blocks * pair_size
    vmem = pl.BlockSpec(memory_space=pltpu.VMEM)
    params = dict(vmem_limit_bytes=50 << 20)
    if share % ROWS:
        cells = spectra.reshape(local_blocks, pair_size, lag_size, share, width)
        cells = lax.dynamic_index_in_dim(cells, lax.axis_index("lag"), 2, keepdims=False)
        moved = lax.all_to_all(cells, "pair", 1, 1, tiled=True).reshape(blocks, share, width)
        rows = -(-share // ROWS) * ROWS
        return pl.pallas_call(
            whiten_kernel,
            out_shape=jax.ShapeDtypeStruct((blocks + 1, rows, width), jnp.bfloat16),
            in_specs=[vmem],
            out_specs=vmem,
            compiler_params=pltpu.CompilerParams(**params),
        )(jnp.pad(moved, ((0, 0), (0, rows - share), (0, 0))))
    white = pl.pallas_call(
        functools.partial(spread_kernel, pair_size, lag_size, share),
        out_shape=jax.ShapeDtypeStruct((local_blocks + 1, pair_size, share, width), jnp.bfloat16),
        in_specs=[pl.BlockSpec(memory_space=pltpu.HBM)],
        out_specs=vmem,
        scratch_shapes=[
            pltpu.VMEM((pair_size, local_blocks, share, width), spectra.dtype),
            pltpu.VMEM((width // 2, width // 2), jnp.bfloat16),
        ]
        + semaphores((pair_size - 1) * CHUNKS),
        compiler_params=pltpu.CompilerParams(collective_id=0, has_side_effects=True, **params),
    )(spectra)
    return white.reshape(blocks + pair_size, share, width)


def place(stacks, pair_size, lag_size, share):
    size = pair_size * lag_size
    groups, _, lags = stacks.shape
    piece = lags // size
    if share % ROWS or piece % 128:
        return lax.all_to_all(stacks[:, :share], ("pair", "lag"), 2, 1, tiled=True)
    return pl.pallas_call(
        functools.partial(place_kernel, size, lag_size, share, piece),
        out_shape=jax.ShapeDtypeStruct((groups, size * share, piece), stacks.dtype),
        in_specs=[pl.BlockSpec(memory_space=pl.ANY)],
        out_specs=pl.BlockSpec(memory_space=pltpu.VMEM),
        scratch_shapes=semaphores(size - 1),
        compiler_params=pltpu.CompilerParams(collective_id=1, has_side_effects=True),
    )(stacks)


def shards(spectra, pair_blocks, live_pairs, stack_group):
    pair_size = lax.axis_size("pair")
    lag_size = lax.axis_size("lag")
    _, _, channels, width = spectra.shape
    share = channels // (pair_size * lag_size)
    owners, slots = stack_group.shape
    even, odd = tables(width // 2)
    if share == ROWS and width == 8 * COLS and pair_size == 4 and lag_size == 2:
        pairs = pair_blocks.transpose(0, 2, 1)
        return fused(
            spectra, pairs, live_pairs, stack_group, even, odd, pair_size, lag_size, share
        )
    white = spread(spectra, pair_size, lag_size, share)
    rows = white.shape[1]
    smem = pl.BlockSpec(memory_space=pltpu.SMEM)
    vmem = pl.BlockSpec(memory_space=pltpu.VMEM)
    ids = pltpu.SMEM((NGRP * (owners * slots + QUAD) + QUAD,), jnp.int32)
    quads = pltpu.SMEM((owners * slots // QUAD + NGRP + BATCH,), jnp.int32)
    stacks = pl.pallas_call(
        kernel,
        out_shape=jax.ShapeDtypeStruct((NGRP, rows, width), jnp.bfloat16),
        in_specs=[smem] * 3 + [vmem] * 3,
        out_specs=vmem,
        scratch_shapes=[
            pltpu.VMEM((BATCH * rows, width), jnp.bfloat16),
            pltpu.VMEM((3, NGRP * rows, width), jnp.float32),
            ids, ids, quads, quads,
            pltpu.SMEM((NGRP,), jnp.int32),
        ],
        compiler_params=pltpu.CompilerParams(vmem_limit_bytes=40 << 20),
    )(
        pair_blocks.transpose(0, 2, 1), live_pairs, stack_group, white, even, odd
    )
    return place(stacks, pair_size, lag_size, share).astype(jnp.float32)


def solution(mesh):
    return jax.shard_map(
        shards,
        mesh=mesh,
        in_specs=(P("win", "pair", "stk", None), P("win", None, None), P("win"), P("win", None)),
        out_specs=P("win", "stk", ("pair", "lag")),
        check_vma=False,
    )
```

```python
import functools
import math

import jax
import jax.numpy as jnp
import numpy as np
from jax import lax
from jax.experimental import pallas as pl
from jax.experimental.pallas import tpu as pltpu
from jax.sharding import PartitionSpec as P

NGRP = 4
HW = 15
AMP_FLOOR = 0.5
EPSILON = 1e-06
ROWS = 16
BATCH = 16
QUAD = 4
CHUNKS = 4
COLS = 128
CHUNK_ROWS = 4
PARTS = 2


def tables(num_bins):
    bins = np.arange(num_bins)[:, None]
    steps = np.arange(num_bins)[None, :]
    angles = (bins * steps % (2 * num_bins)) * (math.pi / num_bins)
    scale = math.sqrt(2.0 / num_bins)
    cosine = np.cos(angles) * scale
    sine = np.sin(angles) * scale
    upper = np.concatenate([cosine, sine], axis=1)
    lower = np.concatenate([-sine, cosine], axis=1)
    even = np.concatenate([upper[0::2], lower[0::2]], axis=0)
    odd = np.concatenate([upper[1::2], lower[1::2]], axis=0)
    shape = (num_bins, 2, num_bins // COLS, COLS)
    even, odd = (t.reshape(shape).swapaxes(1, 2).reshape(t.shape) for t in (even, odd))
    return tuple(jnp.asarray(t, jnp.bfloat16) for t in (even, odd))


def bin_order(bins):
    row = lax.broadcasted_iota(jnp.int32, (bins, bins), 0)
    col = lax.broadcasted_iota(jnp.int32, (bins, bins), 1)
    place = jnp.where(col < bins // 2, 2 * col, 2 * col - (bins - 1))
    return jnp.where(row == place, 1.0, 0.0).astype(jnp.bfloat16)


def kernel(
    pairs, live, groups, white, even_ref, odd_ref, out_ref,
    cross, acc, first_ids, second_ids, quad_at, quad_group, counts,
):
    owners = live.shape[0]
    blocks, (_, rows, width) = white.shape[0] - 1, white.shape
    bins = width // 2
    half = bins // 2

    stride = (first_ids.shape[0] - QUAD) // NGRP

    def add_owner(q, carry):
        def add_slot(s, carry):
            group = groups[q, s]
            count = counts[group]
            at = group * stride + count
            first_ids[at] = pairs[q, 0, s]
            second_ids[at] = pairs[q, 1, s]
            counts[group] = count + 1
            return carry

        return lax.fori_loop(0, live[q], add_slot, carry)

    for g in range(NGRP):
        counts[g] = 0
    lax.fori_loop(0, owners, add_owner, 0)

    def blank(at):
        for i in range(QUAD):
            first_ids[at + i] = blocks
            second_ids[at + i] = blocks

    total = 0
    for g in range(NGRP):
        blank(g * stride + counts[g])

        def add_quad(n, total, g=g):
            quad_at[total] = g * stride + n * QUAD
            quad_group[total] = g
            return total + 1

        total = lax.fori_loop(0, pl.cdiv(counts[g], QUAD), add_quad, total)
    blank(NGRP * stride)
    for i in range(BATCH // QUAD):
        quad_at[total + i] = NGRP * stride
        quad_group[total + i] = 0

    acc[...] = jnp.zeros_like(acc)

    def add_batch(step, carry):
        base = step * (BATCH // QUAD)
        for i in range(BATCH):
            at = quad_at[base + i // QUAD] + i % QUAD
            first = white[first_ids[at]].astype(jnp.float32)
            second = white[second_ids[at]].astype(jnp.float32)
            for n in range(2):
                lo, mid, hi = 2 * n * half, (2 * n + 1) * half, (2 * n + 2) * half
                ra, ia = first[:, lo:mid], first[:, mid:hi]
                rb, ib = second[:, lo:mid], second[:, mid:hi]
                cross[i * rows : (i + 1) * rows, lo:mid] = (ra * rb + ia * ib).astype(jnp.bfloat16)
                cross[i * rows : (i + 1) * rows, mid:hi] = (ia * rb - ra * ib).astype(jnp.bfloat16)
        for col in range(0, bins, COLS):
            def product(n, table):
                both = jnp.dot(
                    cross[:, n * bins : (n + 1) * bins],
                    table[:, 2 * col : 2 * (col + COLS)],
                    preferred_element_type=jnp.float32,
                )
                return both[:, :COLS], both[:, COLS:]

            even_d, even_q = product(0, even_ref)
            odd_d, odd_q = product(1, odd_ref)
            for u in range(BATCH // QUAD):
                start = pl.multiple_of(quad_group[base + u] * rows, rows)
                for side, at in ((-1, col), (1, bins + col)):
                    sums = [0.0, 0.0, 0.0]
                    for i in range(u * QUAD, (u + 1) * QUAD):
                        cut = slice(i * rows, (i + 1) * rows)
                        if side < 0:
                            direct, quad = even_d[cut] - odd_d[cut], even_q[cut] - odd_q[cut]
                        else:
                            direct, quad = even_d[cut] + odd_d[cut], even_q[cut] + odd_q[cut]
                        inverse = jnp.minimum(
                            lax.rsqrt(direct * direct + quad * quad), 1.0 / AMP_FLOOR
                        )
                        terms = (direct, direct * inverse, quad * inverse)
                        sums = [x + y for x, y in zip(sums, terms)]
                    for n, term in enumerate(sums):
                        acc[n, pl.ds(start, rows), at : at + COLS] += term
        return carry

    lax.fori_loop(0, pl.cdiv(total, BATCH // QUAD), add_batch, 0)

    pad = 128
    lags = 2 * bins
    span = lags + pad
    for g in range(NGRP):
        cut = slice(g * rows, (g + 1) * rows)
        root = jnp.sqrt(jnp.full((rows, lags), counts[g].astype(jnp.float32)))
        cosine, sine = acc[1, cut], acc[2, cut]
        coherence = jnp.sqrt(cosine * cosine + sine * sine) / root
        padded = jnp.concatenate([coherence, jnp.zeros((rows, pad), jnp.float32)], axis=1)
        part, smooth, at = padded, padded, 1
        for n in range(1, 5):
            part = part + pltpu.roll(part, span - (1 << (n - 1)), 1)
            smooth = smooth + pltpu.roll(part, span - at, 1)
            at += 1 << n
        smooth = pltpu.roll(smooth, HW, 1)[:, :lags] / (2 * HW + 1)
        out_ref[g] = ((acc[0, cut] / root) * smooth * smooth).astype(out_ref.dtype)


def whiten(values, order):
    bins = values.shape[1] // 2
    half = bins // 2
    values = values.astype(jnp.float32)
    power = jnp.sum(values * values, axis=-1, keepdims=True) * (1.0 / bins)
    whitened = (values / jnp.sqrt(power + EPSILON)).astype(jnp.bfloat16)
    real = jnp.dot(whitened[:, :bins], order, preferred_element_type=jnp.float32)
    imag = jnp.dot(whitened[:, bins:], order, preferred_element_type=jnp.float32)
    parts = (real[:, :half], imag[:, :half], real[:, half:], imag[:, half:])
    return [part.astype(jnp.bfloat16) for part in parts]


def whiten_kernel(spec_ref, out_ref):
    count, rows, width = spec_ref.shape
    half = width // 4
    parts = whiten(spec_ref[...].reshape(count * rows, width), bin_order(width // 2))
    for n, part in enumerate(parts):
        out_ref[:count, :, n * half : (n + 1) * half] = part.reshape(count, rows, half)
    out_ref[count] = jnp.zeros((rows, width), out_ref.dtype)


def greet(partners):
    barrier = pltpu.get_barrier_semaphore()
    for partner in partners:
        pl.semaphore_signal(
            barrier, inc=1, device_id=partner, device_id_type=pl.DeviceIdType.MESH
        )
    pl.semaphore_wait(barrier, len(partners))


def spread_kernel(
    size, lag_size, share, spec_ref, white_ref, held, order_ref, own_sem, send_sem, recv_sem,
):
    local_blocks, _, _, width = spec_ref.shape
    half = width // 4
    me = lax.axis_index("pair")
    lag = lax.axis_index("lag")

    chunk = local_blocks // CHUNKS if local_blocks % CHUNKS == 0 else local_blocks
    chunks = local_blocks // chunk

    def source(target, base, count):
        start = pl.multiple_of((target * lag_size + lag) * share, share)
        return spec_ref.at[base : base + count, 0, pl.ds(start, share), :]

    targets = [lax.rem(me + step, size) for step in range(1, size)]
    greet([{"pair": t} for t in targets])
    copies = {}
    for c in range(chunks):
        for n, target in enumerate(targets):
            copy = pltpu.make_async_remote_copy(
                src_ref=source(target, c * chunk, chunk),
                dst_ref=held.at[n + 1, c * chunk : (c + 1) * chunk],
                send_sem=send_sem.at[n * CHUNKS + c],
                recv_sem=recv_sem.at[n * CHUNKS + c],
                device_id={"pair": target},
                device_id_type=pl.DeviceIdType.MESH,
            )
            copy.start()
            copies[n + 1, c] = copy
    own = pltpu.make_async_copy(source(me, 0, local_blocks), held.at[0], own_sem)
    own.start()
    order_ref[...] = bin_order(width // 2)
    white_ref[local_blocks] = jnp.zeros(white_ref.shape[1:], white_ref.dtype)

    def finish(slot, base):
        origin = lax.rem(me - slot + size, size)
        values = held[slot, base : base + chunk].reshape(chunk * share, width)
        for n, part in enumerate(whiten(values, order_ref[...])):
            white_ref[base : base + chunk, origin, :, n * half : (n + 1) * half] = part.reshape(
                chunk, share, half
            )

    own.wait()
    for c in range(chunks):
        finish(0, c * chunk)
    for c in range(chunks):
        for step in sorted(range(1, size), key=lambda n: min(n, size - n)):
            copies[step, c].wait_recv()
            finish(step, c * chunk)
    for copy in copies.values():
        copy.wait_send()


def place_kernel(size, lag_size, share, piece, stack_ref, out_ref, own_sem, send_sem, recv_sem):
    me = lax.axis_index("pair") * lag_size + lax.axis_index("lag")
    rows = pl.ds(pl.multiple_of(me * share, share), share)

    def source(target):
        return stack_ref.at[:, :, pl.ds(pl.multiple_of(target * piece, piece), piece)]

    targets = [lax.rem(me + step, size) for step in range(1, size)]
    ids = [{"pair": lax.div(t, lag_size), "lag": lax.rem(t, lag_size)} for t in targets]
    greet(ids)
    copies = []
    for n, target in enumerate(targets):
        copy = pltpu.make_async_remote_copy(
            src_ref=source(target),
            dst_ref=out_ref.at[:, rows, :],
            send_sem=send_sem.at[n],
            recv_sem=recv_sem.at[n],
            device_id=ids[n],
            device_id_type=pl.DeviceIdType.MESH,
        )
        copy.start()
        copies.append(copy)
    own = pltpu.make_async_copy(source(me), out_ref.at[:, rows, :], own_sem)
    own.start()
    own.wait()
    for copy in copies:
        copy.wait()


def fused_kernel(
    size, lag_size, spec, pairs_hbm, live_hbm, groups_hbm, even_hbm, odd_hbm, out_ref,
    raw, send, whites, even_ref, odd_ref, order_ref, cross, prefix, stage, got,
    pairs, live, groups, first_ids, second_ids, links, load_sem, table_sem, send_sem, recv_sem, give_sem, take_sem,
):
    local_blocks, _, _, width = spec.shape
    bins = width // 2
    half = bins // 2
    share = raw.shape[2]
    chunks = len(whites)
    devices = size * lag_size
    owners, slots = groups.shape
    quads = prefix.shape[1] - 1
    blank = whites[0].shape[0] - 1
    me = lax.axis_index("pair")
    lag = lax.axis_index("lag")
    place = me * lag_size + lag
    steps = [s for s in (2, 3, 1) if s < size] + [0]

    def device(step):
        return {
            "pair": lax.bitwise_xor(me, step // lag_size),
            "lag": lax.bitwise_xor(lag, step % lag_size),
        }

    barrier = pltpu.get_barrier_semaphore()
    for step in range(1, devices):
        pl.semaphore_signal(
            barrier, inc=1, device_id=device(step), device_id_type=pl.DeviceIdType.MESH
        )
    loads = []
    for n, step in enumerate(steps):
        target = lax.bitwise_xor(me, step)
        start = pl.multiple_of((target * lag_size + lag) * share, share)
        copy = pltpu.make_async_copy(
            spec.at[:, 0, pl.ds(start, share), :], raw.at[n], load_sem.at[n]
        )
        copy.start()
        loads.append(copy)
    fills = [
        pltpu.make_async_copy(even_hbm, even_ref, table_sem.at[0]),
        pltpu.make_async_copy(odd_hbm, odd_ref, table_sem.at[1]),
    ]
    plans = [
        pltpu.make_async_copy(pairs_hbm, pairs, table_sem.at[2]),
        pltpu.make_async_copy(live_hbm, live, table_sem.at[3]),
        pltpu.make_async_copy(groups_hbm, groups, table_sem.at[4]),
    ]
    for copy in plans + fills:
        copy.start()
    order_ref[...] = bin_order(bins)

    low = lax.broadcasted_iota(jnp.int32, (local_blocks, 8, COLS), 1) < 4

    def swap(x):
        return pltpu.roll(x, 4, x.ndim - 2)

    def prepare(n):
        values = raw[n].reshape(local_blocks * share, width).astype(jnp.float32)
        power = jnp.sum(values * values, axis=-1, keepdims=True) * (1.0 / bins)
        whitened = (values * lax.rsqrt(power + EPSILON)).astype(jnp.bfloat16)
        for part in range(2):
            ordered = jnp.dot(
                whitened[:, part * bins : (part + 1) * bins], order_ref[...],
                preferred_element_type=jnp.float32,
            ).reshape(local_blocks, share, bins)
            for v in range(share // 8):
                tiles = [
                    ordered[:, 8 * v : 8 * v + 8, t * COLS : (t + 1) * COLS] for t in range(4)
                ]
                first = [jnp.where(low, tiles[2 * u], swap(tiles[2 * u + 1])) for u in range(2)]
                other = [jnp.where(low, swap(tiles[2 * u]), tiles[2 * u + 1]) for u in range(2)]
                for c, both in ((2 * v, first), (2 * v + 1, other)):
                    block = jnp.concatenate(both, axis=1).astype(jnp.bfloat16)
                    lanes = slice(part * COLS, (part + 1) * COLS)
                    if steps[n]:
                        send[c, n, :, :, lanes] = block
                    else:
                        whites[c][pl.ds(me * local_blocks, local_blocks), :, lanes] = block

    copies = {}

    def give(c, n):
        copy = pltpu.make_async_remote_copy(
            src_ref=send.at[c, n],
            dst_ref=whites[c].at[pl.ds(me * local_blocks, local_blocks)],
            send_sem=send_sem.at[c, n],
            recv_sem=recv_sem.at[c, n],
            device_id=device(steps[n] * lag_size),
            device_id_type=pl.DeviceIdType.MESH,
        )
        copy.start()
        copies[c, n] = copy

    for n in range(size):
        loads[n].wait()
        prepare(n)
        if n == 1:
            pl.semaphore_wait(barrier, devices - 1)
            give(0, 0)
            give(0, 1)
        if n == 2:
            give(0, 2)
            for c in range(1, chunks):
                for m in range(size - 1):
                    give(c, m)
    for white in whites:
        white[blank] = jnp.zeros(white.shape[1:], white.dtype)

    end = owners * slots
    for copy in plans:
        copy.wait()

    def pick(g, values, default):
        for k in range(NGRP):
            default = jnp.where(g == k, values[k], default)
        return default

    def link_owner(p, carry):
        q = owners - 1 - p

        def link_slot(r, carry):
            heads, counts = carry
            s = slots - 1 - r
            g = groups[q, s]
            at = q * slots + s
            links[at] = pick(g, heads, end)
            used = s < live[q]
            hits = [jnp.logical_and(used, g == k) for k in range(NGRP)]
            heads = tuple(jnp.where(h, at, x) for h, x in zip(hits, heads))
            counts = tuple(jnp.where(h, x + 1, x) for h, x in zip(hits, counts))
            return heads, counts

        return lax.fori_loop(0, slots, link_slot, carry)

    zero = jnp.int32(0)
    last = jnp.int32(end)
    heads, counts = lax.fori_loop(0, owners, link_owner, ((last,) * NGRP, (zero,) * NGRP))
    links[end] = last

    def order_quad(n, carry):
        slot, group = carry
        for i in range(QUAD):
            stop = slot == end
            real = jnp.where(stop, 0, slot)
            q = real // slots
            s = real - q * slots

            def row(x):
                return jnp.where(stop, blank, (x % size) * local_blocks + x // size)

            first_ids[n * QUAD + i] = row(pairs[q, 0, s])
            second_ids[n * QUAD + i] = row(pairs[q, 1, s])
            slot = links[slot]
        done = slot == end
        group = jnp.where(done, group + 1, group)
        slot = jnp.where(done, pick(group, heads, last), slot)
        return slot, group

    lax.fori_loop(0, quads, order_quad, (heads[0], zero))
    ends = [zero]
    for k in range(NGRP):
        ends.append(ends[k] + (counts[k] + QUAD - 1) // QUAD)

    for n in range(3):
        prefix[n, 0] = jnp.zeros(prefix.shape[2:], prefix.dtype)
    for copy in fills:
        copy.wait()

    low8 = lax.broadcasted_iota(jnp.int32, (8, COLS), 0) < 4
    part_quads = quads // PARTS
    part_rows = part_quads * 16

    def fill_cross(white):
        def fill_quad(n, carry):
            products = []
            for i in range(QUAD):
                first = white[first_ids[n * QUAD + i]].astype(jnp.float32)
                second = white[second_ids[n * QUAD + i]].astype(jnp.float32)
                ra, ia = first[:, :COLS], first[:, COLS:]
                rb, ib = second[:, :COLS], second[:, COLS:]
                products.append((ra * rb + ia * ib, ia * rb - ra * ib))
            start = pl.multiple_of(n * 16, 16)
            for part in range(2):
                for h in range(2):
                    tops, bottoms = [], []
                    for i in range(0, QUAD, 2):
                        x = products[i][part][8 * h : 8 * h + 8]
                        y = products[i + 1][part][8 * h : 8 * h + 8]
                        tops.append(jnp.where(low8, x, swap(y)))
                        bottoms.append(jnp.where(low8, swap(x), y))
                    for j, tile in enumerate((tops, bottoms)):
                        at = (2 * part + j) * COLS
                        cross[h, pl.ds(start, 16), at : at + COLS] = jnp.concatenate(
                            tile, axis=0
                        ).astype(jnp.bfloat16)
            return carry

        lax.fori_loop(0, quads, fill_quad, 0)

    def add_part(p, carry):
        start = pl.multiple_of(p * part_rows, part_rows)
        base = p * part_quads
        for col in range(0, bins, COLS):
            def product(h, table):
                both = jnp.dot(
                    cross[h, pl.ds(start, part_rows), :],
                    table[:, 2 * col : 2 * (col + COLS)],
                    preferred_element_type=jnp.float32,
                )
                return both[:, :COLS], both[:, COLS:]

            even_d, even_q = product(0, even_ref)
            odd_d, odd_q = product(1, odd_ref)
            for side, at in ((-1, col), (1, bins + col)):
                sums = [prefix[n, base, :, at : at + COLS] for n in range(3)]
                for u in range(part_quads):
                    for i in range(2):
                        cut = slice(u * 16 + i * 8, u * 16 + i * 8 + 8)
                        if side < 0:
                            direct, quad = even_d[cut] - odd_d[cut], even_q[cut] - odd_q[cut]
                        else:
                            direct, quad = even_d[cut] + odd_d[cut], even_q[cut] + odd_q[cut]
                        inverse = jnp.minimum(
                            lax.rsqrt(direct * direct + quad * quad), 1.0 / AMP_FLOOR
                        )
                        terms = (direct, direct * inverse, quad * inverse)
                        sums = [x + y for x, y in zip(sums, terms)]
                    for n in range(3):
                        prefix[n, base + u + 1, :, at : at + COLS] = sums[n]
        return carry

    pad = 128
    lags = 2 * bins
    span = lags + pad
    piece = lags // devices
    low16 = lax.broadcasted_iota(jnp.int32, (8, lags), 0) < 4
    members = []
    for k in range(0, NGRP, 2):
        pair = [jnp.full((8, lags), counts[k + i].astype(jnp.float32)) for i in range(2)]
        members.append(jnp.where(low16, *pair))
    scale = 1.0 / jnp.sqrt(jnp.concatenate(members, axis=0))

    def stack(c):
        totals = []
        for n in range(3):
            rows = []
            for k in range(NGRP):
                total = prefix[n, ends[k + 1]] - prefix[n, ends[k]]
                rows.append(total + swap(total))
            totals.append(
                jnp.concatenate(
                    [jnp.where(low16, rows[k], rows[k + 1]) for k in range(0, NGRP, 2)], axis=0
                )
            )
        linear, cosine, sine = totals
        coherence = jnp.sqrt(cosine * cosine + sine * sine) * scale
        padded = jnp.concatenate([coherence, jnp.zeros((16, pad), jnp.float32)], axis=1)
        part, smooth, at = padded, padded, 1
        for n in range(1, 5):
            part = part + pltpu.roll(part, span - (1 << (n - 1)), 1)
            smooth = smooth + pltpu.roll(part, span - at, 1)
            at += 1 << n
        smooth = pltpu.roll(smooth, HW, 1)[:, :lags] * (1.0 / (2 * HW + 1))
        result = (linear * scale * smooth * smooth).astype(jnp.bfloat16)
        for t in range(devices):
            stage[t, c] = result[:, t * piece : (t + 1) * piece]
        got[place, c] = stage[place, c]

    def give_results(turn, start, count):
        for step in range(devices - 1, 0, -1):
            target = device(step)
            cut = pl.ds(start, count)
            copy = pltpu.make_async_remote_copy(
                src_ref=stage.at[target["pair"] * lag_size + target["lag"], cut],
                dst_ref=got.at[place, cut],
                send_sem=give_sem.at[turn, step - 1],
                recv_sem=take_sem.at[turn, step - 1],
                device_id=target,
                device_id_type=pl.DeviceIdType.MESH,
            )
            copy.start()
            results[turn, step] = copy

    def take_results(turn):
        for step in range(devices - 1, 0, -1):
            results[turn, step].wait_recv()

    low_out = lax.broadcasted_iota(jnp.int32, (devices, 8, piece), 1) < 4

    def assemble(v):
        a = got[:, 2 * v].astype(jnp.float32)
        b = got[:, 2 * v + 1].astype(jnp.float32)
        for k in range(0, NGRP, 2):
            x, y = a[:, 4 * k : 4 * k + 8], b[:, 4 * k : 4 * k + 8]
            out_ref[k, :, 8 * v : 8 * v + 8, :] = jnp.where(low_out, x, swap(y))
            out_ref[k + 1, :, 8 * v : 8 * v + 8, :] = jnp.where(low_out, swap(x), y)

    results = {}
    for c in range(chunks):
        for n in range(size - 1):
            copies[c, n].wait_recv()
        if c == chunks - 1:
            give_results(0, 0, c)
        fill_cross(whites[c])
        lax.fori_loop(0, PARTS, add_part, 0)
        stack(c)
    give_results(1, chunks - 1, 1)
    take_results(0)
    for v in range(chunks // 2 - 1):
        assemble(v)
    take_results(1)
    assemble(chunks // 2 - 1)
    for copy in copies.values():
        copy.wait_send()
    for copy in results.values():
        copy.wait_send()


def fused(spectra, pairs, live, groups, even, odd, pair_size, lag_size, share):
    local_blocks, _, _, width = spectra.shape
    owners, slots = groups.shape
    blocks = local_blocks * pair_size
    devices = pair_size * lag_size
    chunks = share // CHUNK_ROWS
    quads = -(-(owners * slots // QUAD + NGRP) // PARTS) * PARTS
    piece = width // devices
    operands = (spectra, pairs, live, groups, even, odd)
    hbm = pl.BlockSpec(memory_space=pltpu.HBM)
    dma = pltpu.SemaphoreType.DMA
    out = pl.pallas_call(
        functools.partial(fused_kernel, pair_size, lag_size),
        out_shape=jax.ShapeDtypeStruct((NGRP, devices, share, piece), jnp.float32),
        in_specs=[hbm] * 6,
        out_specs=pl.BlockSpec(memory_space=pltpu.VMEM),
        scratch_shapes=[
            pltpu.VMEM((pair_size, local_blocks, share, width), jnp.bfloat16),
            pltpu.VMEM((chunks, pair_size - 1, local_blocks, 16, 2 * COLS), jnp.bfloat16),
            [pltpu.VMEM((blocks + 1, 16, 2 * COLS), jnp.bfloat16)] * chunks,
            pltpu.VMEM(even.shape, jnp.bfloat16),
            pltpu.VMEM(odd.shape, jnp.bfloat16),
            pltpu.VMEM((width // 2, width // 2), jnp.bfloat16),
            pltpu.VMEM((2, quads * 16, width // 2), jnp.bfloat16),
            pltpu.VMEM((3, quads + 1, 8, width), jnp.float32),
            pltpu.VMEM((devices, chunks, 16, piece), jnp.bfloat16),
            pltpu.VMEM((devices, chunks, 16, piece), jnp.bfloat16),
            pltpu.SMEM(pairs.shape, jnp.int32),
            pltpu.SMEM(live.shape, jnp.int32),
            pltpu.SMEM(groups.shape, jnp.int32),
            pltpu.SMEM((quads * QUAD,), jnp.int32),
            pltpu.SMEM((quads * QUAD,), jnp.int32),
            pltpu.SMEM((owners * slots + 1,), jnp.int32),
            dma((pair_size,)),
            dma((5,)),
            dma((chunks, pair_size - 1)),
            dma((chunks, pair_size - 1)),
            dma((2, devices - 1)),
            dma((2, devices - 1)),
        ],
        compiler_params=pltpu.CompilerParams(
            collective_id=2, has_side_effects=True, vmem_limit_bytes=50 << 20
        ),
    )(*(pltpu.with_memory_space_constraint(x, pltpu.HBM) for x in operands))
    return out.reshape(NGRP, devices * share, piece)


def semaphores(count):
    return [
        pltpu.SemaphoreType.DMA,
        pltpu.SemaphoreType.DMA((count,)),
        pltpu.SemaphoreType.DMA((count,)),
    ]


def spread(spectra, pair_size, lag_size, share):
    local_blocks, _, _, width = spectra.shape
    blocks = local_blocks * pair_size
    vmem = pl.BlockSpec(memory_space=pltpu.VMEM)
    params = dict(vmem_limit_bytes=50 << 20)
    if share % ROWS:
        cells = spectra.reshape(local_blocks, pair_size, lag_size, share, width)
        cells = lax.dynamic_index_in_dim(cells, lax.axis_index("lag"), 2, keepdims=False)
        moved = lax.all_to_all(cells, "pair", 1, 1, tiled=True).reshape(blocks, share, width)
        rows = -(-share // ROWS) * ROWS
        return pl.pallas_call(
            whiten_kernel,
            out_shape=jax.ShapeDtypeStruct((blocks + 1, rows, width), jnp.bfloat16),
            in_specs=[vmem],
            out_specs=vmem,
            compiler_params=pltpu.CompilerParams(**params),
        )(jnp.pad(moved, ((0, 0), (0, rows - share), (0, 0))))
    white = pl.pallas_call(
        functools.partial(spread_kernel, pair_size, lag_size, share),
        out_shape=jax.ShapeDtypeStruct((local_blocks + 1, pair_size, share, width), jnp.bfloat16),
        in_specs=[pl.BlockSpec(memory_space=pltpu.HBM)],
        out_specs=vmem,
        scratch_shapes=[
            pltpu.VMEM((pair_size, local_blocks, share, width), spectra.dtype),
            pltpu.VMEM((width // 2, width // 2), jnp.bfloat16),
        ]
        + semaphores((pair_size - 1) * CHUNKS),
        compiler_params=pltpu.CompilerParams(collective_id=0, has_side_effects=True, **params),
    )(spectra)
    return white.reshape(blocks + pair_size, share, width)


def place(stacks, pair_size, lag_size, share):
    size = pair_size * lag_size
    groups, _, lags = stacks.shape
    piece = lags // size
    if share % ROWS or piece % 128:
        return lax.all_to_all(stacks[:, :share], ("pair", "lag"), 2, 1, tiled=True)
    return pl.pallas_call(
        functools.partial(place_kernel, size, lag_size, share, piece),
        out_shape=jax.ShapeDtypeStruct((groups, size * share, piece), stacks.dtype),
        in_specs=[pl.BlockSpec(memory_space=pl.ANY)],
        out_specs=pl.BlockSpec(memory_space=pltpu.VMEM),
        scratch_shapes=semaphores(size - 1),
        compiler_params=pltpu.CompilerParams(collective_id=1, has_side_effects=True),
    )(stacks)


def shards(spectra, pair_blocks, live_pairs, stack_group):
    pair_size = lax.axis_size("pair")
    lag_size = lax.axis_size("lag")
    _, _, channels, width = spectra.shape
    share = channels // (pair_size * lag_size)
    owners, slots = stack_group.shape
    even, odd = tables(width // 2)
    if share == ROWS and width == 8 * COLS and pair_size == 4 and lag_size == 2:
        pairs = pair_blocks.transpose(0, 2, 1)
        return fused(
            spectra, pairs, live_pairs, stack_group, even, odd, pair_size, lag_size, share
        )
    white = spread(spectra, pair_size, lag_size, share)
    rows = white.shape[1]
    smem = pl.BlockSpec(memory_space=pltpu.SMEM)
    vmem = pl.BlockSpec(memory_space=pltpu.VMEM)
    ids = pltpu.SMEM((NGRP * (owners * slots + QUAD) + QUAD,), jnp.int32)
    quads = pltpu.SMEM((owners * slots // QUAD + NGRP + BATCH,), jnp.int32)
    stacks = pl.pallas_call(
        kernel,
        out_shape=jax.ShapeDtypeStruct((NGRP, rows, width), jnp.bfloat16),
        in_specs=[smem] * 3 + [vmem] * 3,
        out_specs=vmem,
        scratch_shapes=[
            pltpu.VMEM((BATCH * rows, width), jnp.bfloat16),
            pltpu.VMEM((3, NGRP * rows, width), jnp.float32),
            ids, ids, quads, quads,
            pltpu.SMEM((NGRP,), jnp.int32),
        ],
        compiler_params=pltpu.CompilerParams(vmem_limit_bytes=40 << 20),
    )(
        pair_blocks.transpose(0, 2, 1), live_pairs, stack_group, white, even, odd
    )
    return place(stacks, pair_size, lag_size, share).astype(jnp.float32)


def solution(mesh):
    return jax.shard_map(
        shards,
        mesh=mesh,
        in_specs=(P("win", "pair", "stk", None), P("win", None, None), P("win"), P("win", None)),
        out_specs=P("win", "stk", ("pair", "lag")),
        check_vma=False,
    )
```

```python
import functools
import math

import jax
import jax.numpy as jnp
import numpy as np
from jax import lax
from jax.experimental import pallas as pl
from jax.experimental.pallas import tpu as pltpu
from jax.sharding import PartitionSpec as P

NGRP = 4
HW = 15
AMP_FLOOR = 0.5
EPSILON = 1e-06
ROWS = 16
BATCH = 16
QUAD = 4
CHUNKS = 4
COLS = 128
CHUNK_ROWS = 4
PARTS = 1


def tables(num_bins):
    bins = np.arange(num_bins)[:, None]
    steps = np.arange(num_bins)[None, :]
    angles = (bins * steps % (2 * num_bins)) * (math.pi / num_bins)
    scale = math.sqrt(2.0 / num_bins)
    cosine = np.cos(angles) * scale
    sine = np.sin(angles) * scale
    upper = np.concatenate([cosine, sine], axis=1)
    lower = np.concatenate([-sine, cosine], axis=1)
    even = np.concatenate([upper[0::2], lower[0::2]], axis=0)
    odd = np.concatenate([upper[1::2], lower[1::2]], axis=0)
    shape = (num_bins, 2, num_bins // COLS, COLS)
    even, odd = (t.reshape(shape).swapaxes(1, 2).reshape(t.shape) for t in (even, odd))
    return tuple(jnp.asarray(t, jnp.bfloat16) for t in (even, odd))


def bin_order(bins):
    row = lax.broadcasted_iota(jnp.int32, (bins, bins), 0)
    col = lax.broadcasted_iota(jnp.int32, (bins, bins), 1)
    place = jnp.where(col < bins // 2, 2 * col, 2 * col - (bins - 1))
    return jnp.where(row == place, 1.0, 0.0).astype(jnp.bfloat16)


def kernel(
    pairs, live, groups, white, even_ref, odd_ref, out_ref,
    cross, acc, first_ids, second_ids, quad_at, quad_group, counts,
):
    owners = live.shape[0]
    blocks, (_, rows, width) = white.shape[0] - 1, white.shape
    bins = width // 2
    half = bins // 2

    stride = (first_ids.shape[0] - QUAD) // NGRP

    def add_owner(q, carry):
        def add_slot(s, carry):
            group = groups[q, s]
            count = counts[group]
            at = group * stride + count
            first_ids[at] = pairs[q, 0, s]
            second_ids[at] = pairs[q, 1, s]
            counts[group] = count + 1
            return carry

        return lax.fori_loop(0, live[q], add_slot, carry)

    for g in range(NGRP):
        counts[g] = 0
    lax.fori_loop(0, owners, add_owner, 0)

    def blank(at):
        for i in range(QUAD):
            first_ids[at + i] = blocks
            second_ids[at + i] = blocks

    total = 0
    for g in range(NGRP):
        blank(g * stride + counts[g])

        def add_quad(n, total, g=g):
            quad_at[total] = g * stride + n * QUAD
            quad_group[total] = g
            return total + 1

        total = lax.fori_loop(0, pl.cdiv(counts[g], QUAD), add_quad, total)
    blank(NGRP * stride)
    for i in range(BATCH // QUAD):
        quad_at[total + i] = NGRP * stride
        quad_group[total + i] = 0

    acc[...] = jnp.zeros_like(acc)

    def add_batch(step, carry):
        base = step * (BATCH // QUAD)
        for i in range(BATCH):
            at = quad_at[base + i // QUAD] + i % QUAD
            first = white[first_ids[at]].astype(jnp.float32)
            second = white[second_ids[at]].astype(jnp.float32)
            for n in range(2):
                lo, mid, hi = 2 * n * half, (2 * n + 1) * half, (2 * n + 2) * half
                ra, ia = first[:, lo:mid], first[:, mid:hi]
                rb, ib = second[:, lo:mid], second[:, mid:hi]
                cross[i * rows : (i + 1) * rows, lo:mid] = (ra * rb + ia * ib).astype(jnp.bfloat16)
                cross[i * rows : (i + 1) * rows, mid:hi] = (ia * rb - ra * ib).astype(jnp.bfloat16)
        for col in range(0, bins, COLS):
            def product(n, table):
                both = jnp.dot(
                    cross[:, n * bins : (n + 1) * bins],
                    table[:, 2 * col : 2 * (col + COLS)],
                    preferred_element_type=jnp.float32,
                )
                return both[:, :COLS], both[:, COLS:]

            even_d, even_q = product(0, even_ref)
            odd_d, odd_q = product(1, odd_ref)
            for u in range(BATCH // QUAD):
                start = pl.multiple_of(quad_group[base + u] * rows, rows)
                for side, at in ((-1, col), (1, bins + col)):
                    sums = [0.0, 0.0, 0.0]
                    for i in range(u * QUAD, (u + 1) * QUAD):
                        cut = slice(i * rows, (i + 1) * rows)
                        if side < 0:
                            direct, quad = even_d[cut] - odd_d[cut], even_q[cut] - odd_q[cut]
                        else:
                            direct, quad = even_d[cut] + odd_d[cut], even_q[cut] + odd_q[cut]
                        inverse = jnp.minimum(
                            lax.rsqrt(direct * direct + quad * quad), 1.0 / AMP_FLOOR
                        )
                        terms = (direct, direct * inverse, quad * inverse)
                        sums = [x + y for x, y in zip(sums, terms)]
                    for n, term in enumerate(sums):
                        acc[n, pl.ds(start, rows), at : at + COLS] += term
        return carry

    lax.fori_loop(0, pl.cdiv(total, BATCH // QUAD), add_batch, 0)

    pad = 128
    lags = 2 * bins
    span = lags + pad
    for g in range(NGRP):
        cut = slice(g * rows, (g + 1) * rows)
        root = jnp.sqrt(jnp.full((rows, lags), counts[g].astype(jnp.float32)))
        cosine, sine = acc[1, cut], acc[2, cut]
        coherence = jnp.sqrt(cosine * cosine + sine * sine) / root
        padded = jnp.concatenate([coherence, jnp.zeros((rows, pad), jnp.float32)], axis=1)
        part, smooth, at = padded, padded, 1
        for n in range(1, 5):
            part = part + pltpu.roll(part, span - (1 << (n - 1)), 1)
            smooth = smooth + pltpu.roll(part, span - at, 1)
            at += 1 << n
        smooth = pltpu.roll(smooth, HW, 1)[:, :lags] / (2 * HW + 1)
        out_ref[g] = ((acc[0, cut] / root) * smooth * smooth).astype(out_ref.dtype)


def whiten(values, order):
    bins = values.shape[1] // 2
    half = bins // 2
    values = values.astype(jnp.float32)
    power = jnp.sum(values * values, axis=-1, keepdims=True) * (1.0 / bins)
    whitened = (values / jnp.sqrt(power + EPSILON)).astype(jnp.bfloat16)
    real = jnp.dot(whitened[:, :bins], order, preferred_element_type=jnp.float32)
    imag = jnp.dot(whitened[:, bins:], order, preferred_element_type=jnp.float32)
    parts = (real[:, :half], imag[:, :half], real[:, half:], imag[:, half:])
    return [part.astype(jnp.bfloat16) for part in parts]


def whiten_kernel(spec_ref, out_ref):
    count, rows, width = spec_ref.shape
    half = width // 4
    parts = whiten(spec_ref[...].reshape(count * rows, width), bin_order(width // 2))
    for n, part in enumerate(parts):
        out_ref[:count, :, n * half : (n + 1) * half] = part.reshape(count, rows, half)
    out_ref[count] = jnp.zeros((rows, width), out_ref.dtype)


def greet(partners):
    barrier = pltpu.get_barrier_semaphore()
    for partner in partners:
        pl.semaphore_signal(
            barrier, inc=1, device_id=partner, device_id_type=pl.DeviceIdType.MESH
        )
    pl.semaphore_wait(barrier, len(partners))


def spread_kernel(
    size, lag_size, share, spec_ref, white_ref, held, order_ref, own_sem, send_sem, recv_sem,
):
    local_blocks, _, _, width = spec_ref.shape
    half = width // 4
    me = lax.axis_index("pair")
    lag = lax.axis_index("lag")

    chunk = local_blocks // CHUNKS if local_blocks % CHUNKS == 0 else local_blocks
    chunks = local_blocks // chunk

    def source(target, base, count):
        start = pl.multiple_of((target * lag_size + lag) * share, share)
        return spec_ref.at[base : base + count, 0, pl.ds(start, share), :]

    targets = [lax.rem(me + step, size) for step in range(1, size)]
    greet([{"pair": t} for t in targets])
    copies = {}
    for c in range(chunks):
        for n, target in enumerate(targets):
            copy = pltpu.make_async_remote_copy(
                src_ref=source(target, c * chunk, chunk),
                dst_ref=held.at[n + 1, c * chunk : (c + 1) * chunk],
                send_sem=send_sem.at[n * CHUNKS + c],
                recv_sem=recv_sem.at[n * CHUNKS + c],
                device_id={"pair": target},
                device_id_type=pl.DeviceIdType.MESH,
            )
            copy.start()
            copies[n + 1, c] = copy
    own = pltpu.make_async_copy(source(me, 0, local_blocks), held.at[0], own_sem)
    own.start()
    order_ref[...] = bin_order(width // 2)
    white_ref[local_blocks] = jnp.zeros(white_ref.shape[1:], white_ref.dtype)

    def finish(slot, base):
        origin = lax.rem(me - slot + size, size)
        values = held[slot, base : base + chunk].reshape(chunk * share, width)
        for n, part in enumerate(whiten(values, order_ref[...])):
            white_ref[base : base + chunk, origin, :, n * half : (n + 1) * half] = part.reshape(
                chunk, share, half
            )

    own.wait()
    for c in range(chunks):
        finish(0, c * chunk)
    for c in range(chunks):
        for step in sorted(range(1, size), key=lambda n: min(n, size - n)):
            copies[step, c].wait_recv()
            finish(step, c * chunk)
    for copy in copies.values():
        copy.wait_send()


def place_kernel(size, lag_size, share, piece, stack_ref, out_ref, own_sem, send_sem, recv_sem):
    me = lax.axis_index("pair") * lag_size + lax.axis_index("lag")
    rows = pl.ds(pl.multiple_of(me * share, share), share)

    def source(target):
        return stack_ref.at[:, :, pl.ds(pl.multiple_of(target * piece, piece), piece)]

    targets = [lax.rem(me + step, size) for step in range(1, size)]
    ids = [{"pair": lax.div(t, lag_size), "lag": lax.rem(t, lag_size)} for t in targets]
    greet(ids)
    copies = []
    for n, target in enumerate(targets):
        copy = pltpu.make_async_remote_copy(
            src_ref=source(target),
            dst_ref=out_ref.at[:, rows, :],
            send_sem=send_sem.at[n],
            recv_sem=recv_sem.at[n],
            device_id=ids[n],
            device_id_type=pl.DeviceIdType.MESH,
        )
        copy.start()
        copies.append(copy)
    own = pltpu.make_async_copy(source(me), out_ref.at[:, rows, :], own_sem)
    own.start()
    own.wait()
    for copy in copies:
        copy.wait()


def fused_kernel(
    size, lag_size, spec, pairs_hbm, live_hbm, groups_hbm, even_hbm, odd_hbm, out_ref,
    raw, send, whites, even_ref, odd_ref, order_ref, cross, prefix, stage, got,
    pairs, live, groups, first_ids, second_ids, links, load_sem, table_sem, send_sem, recv_sem, give_sem, take_sem,
    far_sem, side_sem,
):
    local_blocks, _, _, width = spec.shape
    bins = width // 2
    half = bins // 2
    share = raw.shape[2]
    chunks = len(whites)
    devices = size * lag_size
    owners, slots = groups.shape
    quads = prefix.shape[1] - 1
    blank = whites[0].shape[0] - 1
    me = lax.axis_index("pair")
    lag = lax.axis_index("lag")
    place = me * lag_size + lag
    steps = [3, 2, 1, 0]
    middle = jnp.logical_or(me == 1, me == 2)

    def device(step):
        return {
            "pair": lax.bitwise_xor(me, step // lag_size),
            "lag": lax.bitwise_xor(lag, step % lag_size),
        }

    def signal(sem, step):
        pl.semaphore_signal(
            sem, inc=1, device_id=device(step), device_id_type=pl.DeviceIdType.MESH
        )

    barrier = pltpu.get_barrier_semaphore()
    signal(barrier, 1)
    signal(barrier, lag_size)

    @pl.when(middle)
    def _():
        signal(barrier, 3 * lag_size)

    loads = []
    for n, step in enumerate(steps):
        target = lax.bitwise_xor(me, step)
        start = pl.multiple_of((target * lag_size + lag) * share, share)
        copy = pltpu.make_async_copy(
            spec.at[:, 0, pl.ds(start, share), :], raw.at[n], load_sem.at[n]
        )
        copy.start()
        loads.append(copy)
    fills = [
        pltpu.make_async_copy(even_hbm, even_ref, table_sem.at[0]),
        pltpu.make_async_copy(odd_hbm, odd_ref, table_sem.at[1]),
    ]
    plans = [
        pltpu.make_async_copy(pairs_hbm, pairs, table_sem.at[2]),
        pltpu.make_async_copy(live_hbm, live, table_sem.at[3]),
        pltpu.make_async_copy(groups_hbm, groups, table_sem.at[4]),
    ]
    for copy in plans + fills:
        copy.start()
    order_ref[...] = bin_order(bins)

    low = lax.broadcasted_iota(jnp.int32, (local_blocks, 8, COLS), 1) < 4

    def swap(x):
        return pltpu.roll(x, 4, x.ndim - 2)

    def prepare(n):
        values = raw[n].reshape(local_blocks * share, width).astype(jnp.float32)
        power = jnp.sum(values * values, axis=-1, keepdims=True) * (1.0 / bins)
        whitened = (values * lax.rsqrt(power + EPSILON)).astype(jnp.bfloat16)
        for part in range(2):
            ordered = jnp.dot(
                whitened[:, part * bins : (part + 1) * bins], order_ref[...],
                preferred_element_type=jnp.float32,
            ).reshape(local_blocks, share, bins)
            for v in range(share // 8):
                tiles = [
                    ordered[:, 8 * v : 8 * v + 8, t * COLS : (t + 1) * COLS] for t in range(4)
                ]
                first = [jnp.where(low, tiles[2 * u], swap(tiles[2 * u + 1])) for u in range(2)]
                other = [jnp.where(low, swap(tiles[2 * u]), tiles[2 * u + 1]) for u in range(2)]
                for c, both in ((2 * v, first), (2 * v + 1, other)):
                    block = jnp.concatenate(both, axis=1).astype(jnp.bfloat16)
                    lanes = slice(part * COLS, (part + 1) * COLS)
                    if steps[n]:
                        send[c, n, :, :, lanes] = block
                    else:
                        whites[c][pl.ds(me * local_blocks, local_blocks), :, lanes] = block

    copies = {}

    def give(c, n):
        return pltpu.make_async_remote_copy(
            src_ref=send.at[c, n],
            dst_ref=whites[c].at[pl.ds(me * local_blocks, local_blocks)],
            send_sem=send_sem.at[c, n],
            recv_sem=recv_sem.at[c, n],
            device_id=device(steps[n] * lag_size),
            device_id_type=pl.DeviceIdType.MESH,
        )

    for c in range(chunks):
        for n in range(size - 1):
            copies[c, n] = give(c, n)
    loads[0].wait()
    prepare(0)

    @pl.when(middle)
    def _():
        pl.semaphore_wait(barrier, 3)
        signal(far_sem, 3 * lag_size)
        signal(far_sem, lag_size)
        copies[0, 0].start()

    loads[1].wait()
    prepare(1)

    @pl.when(middle)
    def _():
        pl.semaphore_wait(far_sem, 1)
        signal(far_sem, lag_size)
        copies[0, 1].start()

    @pl.when(jnp.logical_not(middle))
    def _():
        pl.semaphore_wait(barrier, 2)
        pl.semaphore_wait(far_sem, 1)
        copies[0, 1].start()
        pl.semaphore_wait(far_sem, 1)
        copies[0, 0].start()

    signal(side_sem, 1)
    loads[2].wait()
    prepare(2)
    copies[0, 2].start()
    for c in range(1, chunks):
        for n in (1, 0, 2):
            copies[c, n].start()
    loads[3].wait()
    prepare(3)
    for white in whites:
        white[blank] = jnp.zeros(white.shape[1:], white.dtype)

    end = owners * slots
    for copy in plans:
        copy.wait()

    def pick(g, values, default):
        for k in range(NGRP):
            default = jnp.where(g == k, values[k], default)
        return default

    def link_owner(p, carry):
        q = owners - 1 - p

        def link_slot(r, carry):
            heads, counts = carry
            s = slots - 1 - r
            g = groups[q, s]
            at = q * slots + s
            links[at] = pick(g, heads, end)
            used = s < live[q]
            hits = [jnp.logical_and(used, g == k) for k in range(NGRP)]
            heads = tuple(jnp.where(h, at, x) for h, x in zip(hits, heads))
            counts = tuple(jnp.where(h, x + 1, x) for h, x in zip(hits, counts))
            return heads, counts

        return lax.fori_loop(0, slots, link_slot, carry)

    zero = jnp.int32(0)
    last = jnp.int32(end)
    heads, counts = lax.fori_loop(0, owners, link_owner, ((last,) * NGRP, (zero,) * NGRP))
    links[end] = last

    def order_quad(n, carry):
        slot, group = carry
        for i in range(QUAD):
            stop = slot == end
            real = jnp.where(stop, 0, slot)
            q = real // slots
            s = real - q * slots

            def row(x):
                return jnp.where(stop, blank, (x % size) * local_blocks + x // size)

            first_ids[n * QUAD + i] = row(pairs[q, 0, s])
            second_ids[n * QUAD + i] = row(pairs[q, 1, s])
            slot = links[slot]
        done = slot == end
        group = jnp.where(done, group + 1, group)
        slot = jnp.where(done, pick(group, heads, last), slot)
        return slot, group

    lax.fori_loop(0, quads, order_quad, (heads[0], zero))
    ends = [zero]
    for k in range(NGRP):
        ends.append(ends[k] + (counts[k] + QUAD - 1) // QUAD)

    for n in range(3):
        prefix[n, 0] = jnp.zeros(prefix.shape[2:], prefix.dtype)
    for copy in fills:
        copy.wait()

    low8 = lax.broadcasted_iota(jnp.int32, (8, COLS), 0) < 4
    part_quads = quads // PARTS
    part_rows = part_quads * 16

    def fill_cross(white):
        def fill_quad(n, carry):
            products = []
            for i in range(QUAD):
                first = white[first_ids[n * QUAD + i]].astype(jnp.float32)
                second = white[second_ids[n * QUAD + i]].astype(jnp.float32)
                ra, ia = first[:, :COLS], first[:, COLS:]
                rb, ib = second[:, :COLS], second[:, COLS:]
                products.append((ra * rb + ia * ib, ia * rb - ra * ib))
            start = pl.multiple_of(n * 16, 16)
            for part in range(2):
                for h in range(2):
                    tops, bottoms = [], []
                    for i in range(0, QUAD, 2):
                        x = products[i][part][8 * h : 8 * h + 8]
                        y = products[i + 1][part][8 * h : 8 * h + 8]
                        tops.append(jnp.where(low8, x, swap(y)))
                        bottoms.append(jnp.where(low8, swap(x), y))
                    for j, tile in enumerate((tops, bottoms)):
                        at = (2 * part + j) * COLS
                        cross[h, pl.ds(start, 16), at : at + COLS] = jnp.concatenate(
                            tile, axis=0
                        ).astype(jnp.bfloat16)
            return carry

        lax.fori_loop(0, quads, fill_quad, 0, unroll=2)

    def add_part(p, carry):
        start = pl.multiple_of(p * part_rows, part_rows)
        base = p * part_quads
        for col in range(0, bins, COLS):
            def product(h, table):
                both = jnp.dot(
                    cross[h, pl.ds(start, part_rows), :],
                    table[:, 2 * col : 2 * (col + COLS)],
                    preferred_element_type=jnp.float32,
                )
                return both[:, :COLS], both[:, COLS:]

            even_d, even_q = product(0, even_ref)
            odd_d, odd_q = product(1, odd_ref)
            for side, at in ((-1, col), (1, bins + col)):
                sums = [prefix[n, base, :, at : at + COLS] for n in range(3)]
                for u in range(part_quads):
                    for i in range(2):
                        cut = slice(u * 16 + i * 8, u * 16 + i * 8 + 8)
                        if side < 0:
                            direct, quad = even_d[cut] - odd_d[cut], even_q[cut] - odd_q[cut]
                        else:
                            direct, quad = even_d[cut] + odd_d[cut], even_q[cut] + odd_q[cut]
                        inverse = jnp.minimum(
                            lax.rsqrt(direct * direct + quad * quad), 1.0 / AMP_FLOOR
                        )
                        terms = (direct, direct * inverse, quad * inverse)
                        sums = [x + y for x, y in zip(sums, terms)]
                    for n in range(3):
                        prefix[n, base + u + 1, :, at : at + COLS] = sums[n]
        return carry

    pad = 128
    lags = 2 * bins
    span = lags + pad
    piece = lags // devices
    low16 = lax.broadcasted_iota(jnp.int32, (8, lags), 0) < 4
    members = []
    for k in range(0, NGRP, 2):
        pair = [jnp.full((8, lags), counts[k + i].astype(jnp.float32)) for i in range(2)]
        members.append(jnp.where(low16, *pair))
    scale = 1.0 / jnp.sqrt(jnp.concatenate(members, axis=0))

    def stack(c):
        totals = []
        for n in range(3):
            rows = []
            for k in range(NGRP):
                total = prefix[n, ends[k + 1]] - prefix[n, ends[k]]
                rows.append(total + swap(total))
            totals.append(
                jnp.concatenate(
                    [jnp.where(low16, rows[k], rows[k + 1]) for k in range(0, NGRP, 2)], axis=0
                )
            )
        linear, cosine, sine = totals
        coherence = jnp.sqrt(cosine * cosine + sine * sine) * scale
        padded = jnp.concatenate([coherence, jnp.zeros((16, pad), jnp.float32)], axis=1)
        part = padded
        for n in range(4):
            part = part + pltpu.roll(part, 1 << n, 1)
        smooth = (part + pltpu.roll(part, span - HW, 1) - padded)[:, :lags] * (1.0 / (2 * HW + 1))
        result = (linear * scale * smooth * smooth).astype(jnp.bfloat16)
        for t in range(devices):
            stage[t, c] = result[:, t * piece : (t + 1) * piece]
        got[place, c] = stage[place, c]

    def give_results(turn, start, count):
        for step in range(devices - 1, 0, -1):
            target = device(step)
            cut = pl.ds(start, count)
            copy = pltpu.make_async_remote_copy(
                src_ref=stage.at[target["pair"] * lag_size + target["lag"], cut],
                dst_ref=got.at[place, cut],
                send_sem=give_sem.at[turn, step - 1],
                recv_sem=take_sem.at[turn, step - 1],
                device_id=target,
                device_id_type=pl.DeviceIdType.MESH,
            )
            copy.start()
            results[turn, step] = copy

    def take_results(turn):
        for step in range(devices - 1, 0, -1):
            results[turn, step].wait_recv()

    low_out = lax.broadcasted_iota(jnp.int32, (devices, 8, piece), 1) < 4

    def assemble(v):
        a = got[:, 2 * v].astype(jnp.float32)
        b = got[:, 2 * v + 1].astype(jnp.float32)
        for k in range(0, NGRP, 2):
            x, y = a[:, 4 * k : 4 * k + 8], b[:, 4 * k : 4 * k + 8]
            out_ref[k, :, 8 * v : 8 * v + 8, :] = jnp.where(low_out, x, swap(y))
            out_ref[k + 1, :, 8 * v : 8 * v + 8, :] = jnp.where(low_out, swap(x), y)

    results = {}
    for c in range(chunks):
        for n in range(size - 1):
            copies[c, n].wait_recv()
        if c == chunks - 1:
            pl.semaphore_wait(side_sem, 1)
            give_results(0, 0, c)
        fill_cross(whites[c])
        lax.fori_loop(0, PARTS, add_part, 0)
        stack(c)
    give_results(1, chunks - 1, 1)
    take_results(0)
    for v in range(chunks // 2 - 1):
        assemble(v)
    take_results(1)
    assemble(chunks // 2 - 1)
    for copy in copies.values():
        copy.wait_send()
    for copy in results.values():
        copy.wait_send()


def fused(spectra, pairs, live, groups, even, odd, pair_size, lag_size, share):
    local_blocks, _, _, width = spectra.shape
    owners, slots = groups.shape
    blocks = local_blocks * pair_size
    devices = pair_size * lag_size
    chunks = share // CHUNK_ROWS
    quads = -(-(owners * slots // QUAD + NGRP) // PARTS) * PARTS
    piece = width // devices
    operands = (spectra, pairs, live, groups, even, odd)
    hbm = pl.BlockSpec(memory_space=pltpu.HBM)
    dma = pltpu.SemaphoreType.DMA
    out = pl.pallas_call(
        functools.partial(fused_kernel, pair_size, lag_size),
        out_shape=jax.ShapeDtypeStruct((NGRP, devices, share, piece), jnp.float32),
        in_specs=[hbm] * 6,
        out_specs=pl.BlockSpec(memory_space=pltpu.VMEM),
        scratch_shapes=[
            pltpu.VMEM((pair_size, local_blocks, share, width), jnp.bfloat16),
            pltpu.VMEM((chunks, pair_size - 1, local_blocks, 16, 2 * COLS), jnp.bfloat16),
            [pltpu.VMEM((blocks + 1, 16, 2 * COLS), jnp.bfloat16)] * chunks,
            pltpu.VMEM(even.shape, jnp.bfloat16),
            pltpu.VMEM(odd.shape, jnp.bfloat16),
            pltpu.VMEM((width // 2, width // 2), jnp.bfloat16),
            pltpu.VMEM((2, quads * 16, width // 2), jnp.bfloat16),
            pltpu.VMEM((3, quads + 1, 8, width), jnp.float32),
            pltpu.VMEM((devices, chunks, 16, piece), jnp.bfloat16),
            pltpu.VMEM((devices, chunks, 16, piece), jnp.bfloat16),
            pltpu.SMEM(pairs.shape, jnp.int32),
            pltpu.SMEM(live.shape, jnp.int32),
            pltpu.SMEM(groups.shape, jnp.int32),
            pltpu.SMEM((quads * QUAD,), jnp.int32),
            pltpu.SMEM((quads * QUAD,), jnp.int32),
            pltpu.SMEM((owners * slots + 1,), jnp.int32),
            dma((pair_size,)),
            dma((5,)),
            dma((chunks, pair_size - 1)),
            dma((chunks, pair_size - 1)),
            dma((2, devices - 1)),
            dma((2, devices - 1)),
            pltpu.SemaphoreType.REGULAR,
            pltpu.SemaphoreType.REGULAR,
        ],
        compiler_params=pltpu.CompilerParams(
            collective_id=2, has_side_effects=True, vmem_limit_bytes=50 << 20
        ),
    )(*(pltpu.with_memory_space_constraint(x, pltpu.HBM) for x in operands))
    return out.reshape(NGRP, devices * share, piece)


def semaphores(count):
    return [
        pltpu.SemaphoreType.DMA,
        pltpu.SemaphoreType.DMA((count,)),
        pltpu.SemaphoreType.DMA((count,)),
    ]


def spread(spectra, pair_size, lag_size, share):
    local_blocks, _, _, width = spectra.shape
    blocks = local_blocks * pair_size
    vmem = pl.BlockSpec(memory_space=pltpu.VMEM)
    params = dict(vmem_limit_bytes=50 << 20)
    if share % ROWS:
        cells = spectra.reshape(local_blocks, pair_size, lag_size, share, width)
        cells = lax.dynamic_index_in_dim(cells, lax.axis_index("lag"), 2, keepdims=False)
        moved = lax.all_to_all(cells, "pair", 1, 1, tiled=True).reshape(blocks, share, width)
        rows = -(-share // ROWS) * ROWS
        return pl.pallas_call(
            whiten_kernel,
            out_shape=jax.ShapeDtypeStruct((blocks + 1, rows, width), jnp.bfloat16),
            in_specs=[vmem],
            out_specs=vmem,
            compiler_params=pltpu.CompilerParams(**params),
        )(jnp.pad(moved, ((0, 0), (0, rows - share), (0, 0))))
    white = pl.pallas_call(
        functools.partial(spread_kernel, pair_size, lag_size, share),
        out_shape=jax.ShapeDtypeStruct((local_blocks + 1, pair_size, share, width), jnp.bfloat16),
        in_specs=[pl.BlockSpec(memory_space=pltpu.HBM)],
        out_specs=vmem,
        scratch_shapes=[
            pltpu.VMEM((pair_size, local_blocks, share, width), spectra.dtype),
            pltpu.VMEM((width // 2, width // 2), jnp.bfloat16),
        ]
        + semaphores((pair_size - 1) * CHUNKS),
        compiler_params=pltpu.CompilerParams(collective_id=0, has_side_effects=True, **params),
    )(spectra)
    return white.reshape(blocks + pair_size, share, width)


def place(stacks, pair_size, lag_size, share):
    size = pair_size * lag_size
    groups, _, lags = stacks.shape
    piece = lags // size
    if share % ROWS or piece % 128:
        return lax.all_to_all(stacks[:, :share], ("pair", "lag"), 2, 1, tiled=True)
    return pl.pallas_call(
        functools.partial(place_kernel, size, lag_size, share, piece),
        out_shape=jax.ShapeDtypeStruct((groups, size * share, piece), stacks.dtype),
        in_specs=[pl.BlockSpec(memory_space=pl.ANY)],
        out_specs=pl.BlockSpec(memory_space=pltpu.VMEM),
        scratch_shapes=semaphores(size - 1),
        compiler_params=pltpu.CompilerParams(collective_id=1, has_side_effects=True),
    )(stacks)


def shards(spectra, pair_blocks, live_pairs, stack_group):
    pair_size = lax.axis_size("pair")
    lag_size = lax.axis_size("lag")
    _, _, channels, width = spectra.shape
    share = channels // (pair_size * lag_size)
    owners, slots = stack_group.shape
    even, odd = tables(width // 2)
    if share == ROWS and width == 8 * COLS and pair_size == 4 and lag_size == 2:
        pairs = pair_blocks.transpose(0, 2, 1)
        return fused(
            spectra, pairs, live_pairs, stack_group, even, odd, pair_size, lag_size, share
        )
    white = spread(spectra, pair_size, lag_size, share)
    rows = white.shape[1]
    smem = pl.BlockSpec(memory_space=pltpu.SMEM)
    vmem = pl.BlockSpec(memory_space=pltpu.VMEM)
    ids = pltpu.SMEM((NGRP * (owners * slots + QUAD) + QUAD,), jnp.int32)
    quads = pltpu.SMEM((owners * slots // QUAD + NGRP + BATCH,), jnp.int32)
    stacks = pl.pallas_call(
        kernel,
        out_shape=jax.ShapeDtypeStruct((NGRP, rows, width), jnp.bfloat16),
        in_specs=[smem] * 3 + [vmem] * 3,
        out_specs=vmem,
        scratch_shapes=[
            pltpu.VMEM((BATCH * rows, width), jnp.bfloat16),
            pltpu.VMEM((3, NGRP * rows, width), jnp.float32),
            ids, ids, quads, quads,
            pltpu.SMEM((NGRP,), jnp.int32),
        ],
        compiler_params=pltpu.CompilerParams(vmem_limit_bytes=40 << 20),
    )(
        pair_blocks.transpose(0, 2, 1), live_pairs, stack_group, white, even, odd
    )
    return place(stacks, pair_size, lag_size, share).astype(jnp.float32)


def solution(mesh):
    return jax.shard_map(
        shards,
        mesh=mesh,
        in_specs=(P("win", "pair", "stk", None), P("win", None, None), P("win"), P("win", None)),
        out_specs=P("win", "stk", ("pair", "lag")),
        check_vma=False,
    )
```

```python
import functools
import math

import jax
import jax.numpy as jnp
import numpy as np
from jax import lax
from jax.experimental import pallas as pl
from jax.experimental.pallas import tpu as pltpu
from jax.sharding import PartitionSpec as P

NGRP = 4
HW = 15
AMP_FLOOR = 0.5
EPSILON = 1e-06
ROWS = 16
BATCH = 16
QUAD = 4
CHUNKS = 4
COLS = 128
CHUNK_ROWS = 4
PARTS = 1


def tables(num_bins):
    bins = np.arange(num_bins)[:, None]
    steps = np.arange(num_bins)[None, :]
    angles = (bins * steps % (2 * num_bins)) * (math.pi / num_bins)
    scale = math.sqrt(2.0 / num_bins)
    cosine = np.cos(angles) * scale
    sine = np.sin(angles) * scale
    upper = np.concatenate([cosine, sine], axis=1)
    lower = np.concatenate([-sine, cosine], axis=1)
    even = np.concatenate([upper[0::2], lower[0::2]], axis=0)
    odd = np.concatenate([upper[1::2], lower[1::2]], axis=0)
    shape = (num_bins, 2, num_bins // COLS, COLS)
    even, odd = (t.reshape(shape).swapaxes(1, 2).reshape(t.shape) for t in (even, odd))
    return tuple(jnp.asarray(t, jnp.bfloat16) for t in (even, odd))


def bin_order(bins):
    row = lax.broadcasted_iota(jnp.int32, (bins, bins), 0)
    col = lax.broadcasted_iota(jnp.int32, (bins, bins), 1)
    place = jnp.where(col < bins // 2, 2 * col, 2 * col - (bins - 1))
    return jnp.where(row == place, 1.0, 0.0).astype(jnp.bfloat16)


def kernel(
    pairs, live, groups, white, even_ref, odd_ref, out_ref,
    cross, acc, first_ids, second_ids, quad_at, quad_group, counts,
):
    owners = live.shape[0]
    blocks, (_, rows, width) = white.shape[0] - 1, white.shape
    bins = width // 2
    half = bins // 2

    stride = (first_ids.shape[0] - QUAD) // NGRP

    def add_owner(q, carry):
        def add_slot(s, carry):
            group = groups[q, s]
            count = counts[group]
            at = group * stride + count
            first_ids[at] = pairs[q, 0, s]
            second_ids[at] = pairs[q, 1, s]
            counts[group] = count + 1
            return carry

        return lax.fori_loop(0, live[q], add_slot, carry)

    for g in range(NGRP):
        counts[g] = 0
    lax.fori_loop(0, owners, add_owner, 0)

    def blank(at):
        for i in range(QUAD):
            first_ids[at + i] = blocks
            second_ids[at + i] = blocks

    total = 0
    for g in range(NGRP):
        blank(g * stride + counts[g])

        def add_quad(n, total, g=g):
            quad_at[total] = g * stride + n * QUAD
            quad_group[total] = g
            return total + 1

        total = lax.fori_loop(0, pl.cdiv(counts[g], QUAD), add_quad, total)
    blank(NGRP * stride)
    for i in range(BATCH // QUAD):
        quad_at[total + i] = NGRP * stride
        quad_group[total + i] = 0

    acc[...] = jnp.zeros_like(acc)

    def add_batch(step, carry):
        base = step * (BATCH // QUAD)
        for i in range(BATCH):
            at = quad_at[base + i // QUAD] + i % QUAD
            first = white[first_ids[at]].astype(jnp.float32)
            second = white[second_ids[at]].astype(jnp.float32)
            for n in range(2):
                lo, mid, hi = 2 * n * half, (2 * n + 1) * half, (2 * n + 2) * half
                ra, ia = first[:, lo:mid], first[:, mid:hi]
                rb, ib = second[:, lo:mid], second[:, mid:hi]
                cross[i * rows : (i + 1) * rows, lo:mid] = (ra * rb + ia * ib).astype(jnp.bfloat16)
                cross[i * rows : (i + 1) * rows, mid:hi] = (ia * rb - ra * ib).astype(jnp.bfloat16)
        for col in range(0, bins, COLS):
            def product(n, table):
                both = jnp.dot(
                    cross[:, n * bins : (n + 1) * bins],
                    table[:, 2 * col : 2 * (col + COLS)],
                    preferred_element_type=jnp.float32,
                )
                return both[:, :COLS], both[:, COLS:]

            even_d, even_q = product(0, even_ref)
            odd_d, odd_q = product(1, odd_ref)
            for u in range(BATCH // QUAD):
                start = pl.multiple_of(quad_group[base + u] * rows, rows)
                for side, at in ((-1, col), (1, bins + col)):
                    sums = [0.0, 0.0, 0.0]
                    for i in range(u * QUAD, (u + 1) * QUAD):
                        cut = slice(i * rows, (i + 1) * rows)
                        if side < 0:
                            direct, quad = even_d[cut] - odd_d[cut], even_q[cut] - odd_q[cut]
                        else:
                            direct, quad = even_d[cut] + odd_d[cut], even_q[cut] + odd_q[cut]
                        inverse = jnp.minimum(
                            lax.rsqrt(direct * direct + quad * quad), 1.0 / AMP_FLOOR
                        )
                        terms = (direct, direct * inverse, quad * inverse)
                        sums = [x + y for x, y in zip(sums, terms)]
                    for n, term in enumerate(sums):
                        acc[n, pl.ds(start, rows), at : at + COLS] += term
        return carry

    lax.fori_loop(0, pl.cdiv(total, BATCH // QUAD), add_batch, 0)

    pad = 128
    lags = 2 * bins
    span = lags + pad
    for g in range(NGRP):
        cut = slice(g * rows, (g + 1) * rows)
        root = jnp.sqrt(jnp.full((rows, lags), counts[g].astype(jnp.float32)))
        cosine, sine = acc[1, cut], acc[2, cut]
        coherence = jnp.sqrt(cosine * cosine + sine * sine) / root
        padded = jnp.concatenate([coherence, jnp.zeros((rows, pad), jnp.float32)], axis=1)
        part, smooth, at = padded, padded, 1
        for n in range(1, 5):
            part = part + pltpu.roll(part, span - (1 << (n - 1)), 1)
            smooth = smooth + pltpu.roll(part, span - at, 1)
            at += 1 << n
        smooth = pltpu.roll(smooth, HW, 1)[:, :lags] / (2 * HW + 1)
        out_ref[g] = ((acc[0, cut] / root) * smooth * smooth).astype(out_ref.dtype)


def whiten(values, order):
    bins = values.shape[1] // 2
    half = bins // 2
    values = values.astype(jnp.float32)
    power = jnp.sum(values * values, axis=-1, keepdims=True) * (1.0 / bins)
    whitened = (values / jnp.sqrt(power + EPSILON)).astype(jnp.bfloat16)
    real = jnp.dot(whitened[:, :bins], order, preferred_element_type=jnp.float32)
    imag = jnp.dot(whitened[:, bins:], order, preferred_element_type=jnp.float32)
    parts = (real[:, :half], imag[:, :half], real[:, half:], imag[:, half:])
    return [part.astype(jnp.bfloat16) for part in parts]


def whiten_kernel(spec_ref, out_ref):
    count, rows, width = spec_ref.shape
    half = width // 4
    parts = whiten(spec_ref[...].reshape(count * rows, width), bin_order(width // 2))
    for n, part in enumerate(parts):
        out_ref[:count, :, n * half : (n + 1) * half] = part.reshape(count, rows, half)
    out_ref[count] = jnp.zeros((rows, width), out_ref.dtype)


def greet(partners):
    barrier = pltpu.get_barrier_semaphore()
    for partner in partners:
        pl.semaphore_signal(
            barrier, inc=1, device_id=partner, device_id_type=pl.DeviceIdType.MESH
        )
    pl.semaphore_wait(barrier, len(partners))


def spread_kernel(
    size, lag_size, share, spec_ref, white_ref, held, order_ref, own_sem, send_sem, recv_sem,
):
    local_blocks, _, _, width = spec_ref.shape
    half = width // 4
    me = lax.axis_index("pair")
    lag = lax.axis_index("lag")

    chunk = local_blocks // CHUNKS if local_blocks % CHUNKS == 0 else local_blocks
    chunks = local_blocks // chunk

    def source(target, base, count):
        start = pl.multiple_of((target * lag_size + lag) * share, share)
        return spec_ref.at[base : base + count, 0, pl.ds(start, share), :]

    targets = [lax.rem(me + step, size) for step in range(1, size)]
    greet([{"pair": t} for t in targets])
    copies = {}
    for c in range(chunks):
        for n, target in enumerate(targets):
            copy = pltpu.make_async_remote_copy(
                src_ref=source(target, c * chunk, chunk),
                dst_ref=held.at[n + 1, c * chunk : (c + 1) * chunk],
                send_sem=send_sem.at[n * CHUNKS + c],
                recv_sem=recv_sem.at[n * CHUNKS + c],
                device_id={"pair": target},
                device_id_type=pl.DeviceIdType.MESH,
            )
            copy.start()
            copies[n + 1, c] = copy
    own = pltpu.make_async_copy(source(me, 0, local_blocks), held.at[0], own_sem)
    own.start()
    order_ref[...] = bin_order(width // 2)
    white_ref[local_blocks] = jnp.zeros(white_ref.shape[1:], white_ref.dtype)

    def finish(slot, base):
        origin = lax.rem(me - slot + size, size)
        values = held[slot, base : base + chunk].reshape(chunk * share, width)
        for n, part in enumerate(whiten(values, order_ref[...])):
            white_ref[base : base + chunk, origin, :, n * half : (n + 1) * half] = part.reshape(
                chunk, share, half
            )

    own.wait()
    for c in range(chunks):
        finish(0, c * chunk)
    for c in range(chunks):
        for step in sorted(range(1, size), key=lambda n: min(n, size - n)):
            copies[step, c].wait_recv()
            finish(step, c * chunk)
    for copy in copies.values():
        copy.wait_send()


def place_kernel(size, lag_size, share, piece, stack_ref, out_ref, own_sem, send_sem, recv_sem):
    me = lax.axis_index("pair") * lag_size + lax.axis_index("lag")
    rows = pl.ds(pl.multiple_of(me * share, share), share)

    def source(target):
        return stack_ref.at[:, :, pl.ds(pl.multiple_of(target * piece, piece), piece)]

    targets = [lax.rem(me + step, size) for step in range(1, size)]
    ids = [{"pair": lax.div(t, lag_size), "lag": lax.rem(t, lag_size)} for t in targets]
    greet(ids)
    copies = []
    for n, target in enumerate(targets):
        copy = pltpu.make_async_remote_copy(
            src_ref=source(target),
            dst_ref=out_ref.at[:, rows, :],
            send_sem=send_sem.at[n],
            recv_sem=recv_sem.at[n],
            device_id=ids[n],
            device_id_type=pl.DeviceIdType.MESH,
        )
        copy.start()
        copies.append(copy)
    own = pltpu.make_async_copy(source(me), out_ref.at[:, rows, :], own_sem)
    own.start()
    own.wait()
    for copy in copies:
        copy.wait()


def fused_kernel(
    size, lag_size, spec, pairs_hbm, live_hbm, groups_hbm, even_hbm, odd_hbm, out_ref,
    raw, send, whites, even_ref, odd_ref, order_ref, cross, prefix, stage, got,
    pairs, live, groups, first_ids, second_ids, links, load_sem, table_sem, send_sem, recv_sem, give_sem, take_sem,
    far_sem, side_sem,
):
    local_blocks, _, _, width = spec.shape
    bins = width // 2
    half = bins // 2
    share = raw.shape[2]
    chunks = len(whites)
    devices = size * lag_size
    owners, slots = groups.shape
    quads = prefix.shape[1] - 1
    blank = whites[0].shape[0] - 1
    me = lax.axis_index("pair")
    lag = lax.axis_index("lag")
    place = me * lag_size + lag
    steps = [3, 2, 1, 0]
    middle = jnp.logical_or(me == 1, me == 2)

    def device(step):
        return {
            "pair": lax.bitwise_xor(me, step // lag_size),
            "lag": lax.bitwise_xor(lag, step % lag_size),
        }

    def signal(sem, step):
        pl.semaphore_signal(
            sem, inc=1, device_id=device(step), device_id_type=pl.DeviceIdType.MESH
        )

    barrier = pltpu.get_barrier_semaphore()
    signal(barrier, 1)
    signal(barrier, lag_size)

    @pl.when(middle)
    def _():
        signal(barrier, 3 * lag_size)

    loads = []
    for n, step in enumerate(steps):
        target = lax.bitwise_xor(me, step)
        start = pl.multiple_of((target * lag_size + lag) * share, share)
        copy = pltpu.make_async_copy(
            spec.at[:, 0, pl.ds(start, share), :], raw.at[n], load_sem.at[n]
        )
        copy.start()
        loads.append(copy)
    fills = [
        pltpu.make_async_copy(even_hbm, even_ref, table_sem.at[0]),
        pltpu.make_async_copy(odd_hbm, odd_ref, table_sem.at[1]),
    ]
    plans = [
        pltpu.make_async_copy(pairs_hbm, pairs, table_sem.at[2]),
        pltpu.make_async_copy(live_hbm, live, table_sem.at[3]),
        pltpu.make_async_copy(groups_hbm, groups, table_sem.at[4]),
    ]
    for copy in plans + fills:
        copy.start()
    order_ref[...] = bin_order(bins)

    low = lax.broadcasted_iota(jnp.int32, (local_blocks, 8, COLS), 1) < 4

    def swap(x):
        return pltpu.roll(x, 4, x.ndim - 2)

    def prepare(n):
        values = raw[n].reshape(local_blocks * share, width).astype(jnp.float32)
        power = jnp.sum(values * values, axis=-1, keepdims=True) * (1.0 / bins)
        whitened = (values * lax.rsqrt(power + EPSILON)).astype(jnp.bfloat16)
        for part in range(2):
            ordered = jnp.dot(
                whitened[:, part * bins : (part + 1) * bins], order_ref[...],
                preferred_element_type=jnp.float32,
            ).reshape(local_blocks, share, bins)
            for v in range(share // 8):
                tiles = [
                    ordered[:, 8 * v : 8 * v + 8, t * COLS : (t + 1) * COLS] for t in range(4)
                ]
                first = [jnp.where(low, tiles[2 * u], swap(tiles[2 * u + 1])) for u in range(2)]
                other = [jnp.where(low, swap(tiles[2 * u]), tiles[2 * u + 1]) for u in range(2)]
                for c, both in ((2 * v, first), (2 * v + 1, other)):
                    block = jnp.concatenate(both, axis=1).astype(jnp.bfloat16)
                    lanes = slice(part * COLS, (part + 1) * COLS)
                    if steps[n]:
                        send[c, n, :, :, lanes] = block
                    else:
                        whites[c][pl.ds(me * local_blocks, local_blocks), :, lanes] = block

    copies = {}

    def give(c, n):
        return pltpu.make_async_remote_copy(
            src_ref=send.at[c, n],
            dst_ref=whites[c].at[pl.ds(me * local_blocks, local_blocks)],
            send_sem=send_sem.at[c, n],
            recv_sem=recv_sem.at[c, n],
            device_id=device(steps[n] * lag_size),
            device_id_type=pl.DeviceIdType.MESH,
        )

    for c in range(chunks):
        for n in range(size - 1):
            copies[c, n] = give(c, n)
    loads[0].wait()
    prepare(0)

    @pl.when(middle)
    def _():
        pl.semaphore_wait(barrier, 3)
        signal(far_sem, 3 * lag_size)
        signal(far_sem, lag_size)
        copies[0, 0].start()

    loads[1].wait()
    prepare(1)

    @pl.when(middle)
    def _():
        pl.semaphore_wait(far_sem, 1)
        signal(far_sem, lag_size)
        copies[0, 1].start()

    @pl.when(jnp.logical_not(middle))
    def _():
        pl.semaphore_wait(barrier, 2)
        pl.semaphore_wait(far_sem, 1)
        copies[0, 1].start()
        pl.semaphore_wait(far_sem, 1)
        copies[0, 0].start()

    signal(side_sem, 1)
    loads[2].wait()
    prepare(2)
    copies[0, 2].start()
    for c in range(1, chunks):
        for n in (1, 0, 2):
            copies[c, n].start()
    loads[3].wait()
    prepare(3)
    for white in whites:
        white[blank] = jnp.zeros(white.shape[1:], white.dtype)

    end = owners * slots
    for copy in plans:
        copy.wait()

    def pick(g, values, default):
        for k in range(NGRP):
            default = jnp.where(g == k, values[k], default)
        return default

    def link_owner(p, carry):
        q = owners - 1 - p

        def link_slot(r, carry):
            heads, counts = carry
            s = slots - 1 - r
            g = groups[q, s]
            at = q * slots + s
            links[at] = pick(g, heads, end)
            used = s < live[q]
            hits = [jnp.logical_and(used, g == k) for k in range(NGRP)]
            heads = tuple(jnp.where(h, at, x) for h, x in zip(hits, heads))
            counts = tuple(jnp.where(h, x + 1, x) for h, x in zip(hits, counts))
            return heads, counts

        return lax.fori_loop(0, slots, link_slot, carry)

    zero = jnp.int32(0)
    last = jnp.int32(end)
    heads, counts = lax.fori_loop(0, owners, link_owner, ((last,) * NGRP, (zero,) * NGRP))
    links[end] = last

    def order_quad(n, carry):
        slot, group = carry
        for i in range(QUAD):
            stop = slot == end
            real = jnp.where(stop, 0, slot)
            q = real // slots
            s = real - q * slots

            def row(x):
                return jnp.where(stop, blank, (x % size) * local_blocks + x // size)

            first_ids[n * QUAD + i] = row(pairs[q, 0, s])
            second_ids[n * QUAD + i] = row(pairs[q, 1, s])
            slot = links[slot]
        done = slot == end
        group = jnp.where(done, group + 1, group)
        slot = jnp.where(done, pick(group, heads, last), slot)
        return slot, group

    lax.fori_loop(0, quads, order_quad, (heads[0], zero))
    ends = [zero]
    for k in range(NGRP):
        ends.append(ends[k] + (counts[k] + QUAD - 1) // QUAD)

    for n in range(3):
        prefix[n, 0] = jnp.zeros(prefix.shape[2:], prefix.dtype)
    for copy in fills:
        copy.wait()

    low8 = lax.broadcasted_iota(jnp.int32, (8, COLS), 0) < 4
    part_quads = quads // PARTS
    part_rows = part_quads * 16

    def fill_cross(white):
        def fill_quad(n, carry):
            products = []
            for i in range(QUAD):
                first = white[first_ids[n * QUAD + i]].astype(jnp.float32)
                second = white[second_ids[n * QUAD + i]].astype(jnp.float32)
                ra, ia = first[:, :COLS], first[:, COLS:]
                rb, ib = second[:, :COLS], second[:, COLS:]
                products.append((ra * rb + ia * ib, ia * rb - ra * ib))
            start = pl.multiple_of(n * 16, 16)
            for part in range(2):
                for h in range(2):
                    tops, bottoms = [], []
                    for i in range(0, QUAD, 2):
                        x = products[i][part][8 * h : 8 * h + 8]
                        y = products[i + 1][part][8 * h : 8 * h + 8]
                        tops.append(jnp.where(low8, x, swap(y)))
                        bottoms.append(jnp.where(low8, swap(x), y))
                    for j, tile in enumerate((tops, bottoms)):
                        at = (2 * part + j) * COLS
                        cross[h, pl.ds(start, 16), at : at + COLS] = jnp.concatenate(
                            tile, axis=0
                        ).astype(jnp.bfloat16)
            return carry

        lax.fori_loop(0, quads, fill_quad, 0, unroll=2)

    def add_part(p, carry):
        start = pl.multiple_of(p * part_rows, part_rows)
        base = p * part_quads
        for col in range(0, bins, COLS):
            def product(h, table):
                both = jnp.dot(
                    cross[h, pl.ds(start, part_rows), :],
                    table[:, 2 * col : 2 * (col + COLS)],
                    preferred_element_type=jnp.float32,
                )
                return both[:, :COLS], both[:, COLS:]

            even_d, even_q = product(0, even_ref)
            odd_d, odd_q = product(1, odd_ref)
            for side, at in ((-1, col), (1, bins + col)):
                sums = [prefix[n, base, :, at : at + COLS] for n in range(3)]
                for u in range(part_quads):
                    for i in range(2):
                        cut = slice(u * 16 + i * 8, u * 16 + i * 8 + 8)
                        if side < 0:
                            direct, quad = even_d[cut] - odd_d[cut], even_q[cut] - odd_q[cut]
                        else:
                            direct, quad = even_d[cut] + odd_d[cut], even_q[cut] + odd_q[cut]
                        inverse = jnp.minimum(
                            lax.rsqrt(direct * direct + quad * quad), 1.0 / AMP_FLOOR
                        )
                        terms = (direct, direct * inverse, quad * inverse)
                        sums = [x + y for x, y in zip(sums, terms)]
                    for n in range(3):
                        prefix[n, base + u + 1, :, at : at + COLS] = sums[n]
        return carry

    pad = 128
    lags = 2 * bins
    span = lags + pad
    piece = lags // devices
    low16 = lax.broadcasted_iota(jnp.int32, (8, lags), 0) < 4
    members = []
    for k in range(0, NGRP, 2):
        pair = [jnp.full((8, lags), counts[k + i].astype(jnp.float32)) for i in range(2)]
        members.append(jnp.where(low16, *pair))
    scale = 1.0 / jnp.sqrt(jnp.concatenate(members, axis=0))

    def stack(c):
        totals = []
        for n in range(3):
            rows = []
            for k in range(NGRP):
                total = prefix[n, ends[k + 1]] - prefix[n, ends[k]]
                rows.append(total + swap(total))
            totals.append(
                jnp.concatenate(
                    [jnp.where(low16, rows[k], rows[k + 1]) for k in range(0, NGRP, 2)], axis=0
                )
            )
        linear, cosine, sine = totals
        coherence = jnp.sqrt(cosine * cosine + sine * sine) * scale
        padded = jnp.concatenate([coherence, jnp.zeros((16, pad), jnp.float32)], axis=1)
        part = padded
        for n in range(4):
            part = part + pltpu.roll(part, 1 << n, 1)
        smooth = (part + pltpu.roll(part, span - HW, 1) - padded)[:, :lags] * (1.0 / (2 * HW + 1))
        result = (linear * scale * smooth * smooth).astype(jnp.bfloat16)
        for t in range(devices):
            stage[t, c] = result[:, t * piece : (t + 1) * piece]
        got[place, c] = stage[place, c]

    def give_results(turn, start, count, order=(5, 4, 7, 6, 3, 2, 1)):
        for step in order:
            target = device(step)
            cut = pl.ds(start, count)
            copy = pltpu.make_async_remote_copy(
                src_ref=stage.at[target["pair"] * lag_size + target["lag"], cut],
                dst_ref=got.at[place, cut],
                send_sem=give_sem.at[turn, step - 1],
                recv_sem=take_sem.at[turn, step - 1],
                device_id=target,
                device_id_type=pl.DeviceIdType.MESH,
            )
            copy.start()
            results[turn, step] = copy

    def take_results(turn):
        for step in range(devices - 1, 0, -1):
            results[turn, step].wait_recv()

    low_out = lax.broadcasted_iota(jnp.int32, (devices, 8, piece), 1) < 4

    def assemble(v):
        a = got[:, 2 * v].astype(jnp.float32)
        b = got[:, 2 * v + 1].astype(jnp.float32)
        for k in range(0, NGRP, 2):
            x, y = a[:, 4 * k : 4 * k + 8], b[:, 4 * k : 4 * k + 8]
            out_ref[k, :, 8 * v : 8 * v + 8, :] = jnp.where(low_out, x, swap(y))
            out_ref[k + 1, :, 8 * v : 8 * v + 8, :] = jnp.where(low_out, swap(x), y)

    results = {}
    for c in range(chunks):
        for n in range(size - 1):
            copies[c, n].wait_recv()
        fill_cross(whites[c])
        if c == chunks - 1:
            give_results(0, 0, c, (5, 4, 7, 6))
        lax.fori_loop(0, PARTS, add_part, 0)
        stack(c)
        if c == chunks - 2:
            pl.semaphore_wait(side_sem, 1)
            give_results(0, 0, chunks - 1, (3, 2, 1))
    give_results(1, chunks - 1, 1)
    take_results(0)
    for v in range(chunks // 2 - 1):
        assemble(v)
    take_results(1)
    assemble(chunks // 2 - 1)
    for copy in copies.values():
        copy.wait_send()
    for copy in results.values():
        copy.wait_send()


def fused(spectra, pairs, live, groups, even, odd, pair_size, lag_size, share):
    local_blocks, _, _, width = spectra.shape
    owners, slots = groups.shape
    blocks = local_blocks * pair_size
    devices = pair_size * lag_size
    chunks = share // CHUNK_ROWS
    quads = -(-(owners * slots // QUAD + NGRP) // PARTS) * PARTS
    piece = width // devices
    operands = (spectra, pairs, live, groups, even, odd)
    hbm = pl.BlockSpec(memory_space=pltpu.HBM)
    dma = pltpu.SemaphoreType.DMA
    out = pl.pallas_call(
        functools.partial(fused_kernel, pair_size, lag_size),
        out_shape=jax.ShapeDtypeStruct((NGRP, devices, share, piece), jnp.float32),
        in_specs=[hbm] * 6,
        out_specs=pl.BlockSpec(memory_space=pltpu.VMEM),
        scratch_shapes=[
            pltpu.VMEM((pair_size, local_blocks, share, width), jnp.bfloat16),
            pltpu.VMEM((chunks, pair_size - 1, local_blocks, 16, 2 * COLS), jnp.bfloat16),
            [pltpu.VMEM((blocks + 1, 16, 2 * COLS), jnp.bfloat16)] * chunks,
            pltpu.VMEM(even.shape, jnp.bfloat16),
            pltpu.VMEM(odd.shape, jnp.bfloat16),
            pltpu.VMEM((width // 2, width // 2), jnp.bfloat16),
            pltpu.VMEM((2, quads * 16, width // 2), jnp.bfloat16),
            pltpu.VMEM((3, quads + 1, 8, width), jnp.float32),
            pltpu.VMEM((devices, chunks, 16, piece), jnp.bfloat16),
            pltpu.VMEM((devices, chunks, 16, piece), jnp.bfloat16),
            pltpu.SMEM(pairs.shape, jnp.int32),
            pltpu.SMEM(live.shape, jnp.int32),
            pltpu.SMEM(groups.shape, jnp.int32),
            pltpu.SMEM((quads * QUAD,), jnp.int32),
            pltpu.SMEM((quads * QUAD,), jnp.int32),
            pltpu.SMEM((owners * slots + 1,), jnp.int32),
            dma((pair_size,)),
            dma((5,)),
            dma((chunks, pair_size - 1)),
            dma((chunks, pair_size - 1)),
            dma((2, devices - 1)),
            dma((2, devices - 1)),
            pltpu.SemaphoreType.REGULAR,
            pltpu.SemaphoreType.REGULAR,
        ],
        compiler_params=pltpu.CompilerParams(
            collective_id=2, has_side_effects=True, vmem_limit_bytes=50 << 20
        ),
    )(*(pltpu.with_memory_space_constraint(x, pltpu.HBM) for x in operands))
    return out.reshape(NGRP, devices * share, piece)


def semaphores(count):
    return [
        pltpu.SemaphoreType.DMA,
        pltpu.SemaphoreType.DMA((count,)),
        pltpu.SemaphoreType.DMA((count,)),
    ]


def spread(spectra, pair_size, lag_size, share):
    local_blocks, _, _, width = spectra.shape
    blocks = local_blocks * pair_size
    vmem = pl.BlockSpec(memory_space=pltpu.VMEM)
    params = dict(vmem_limit_bytes=50 << 20)
    if share % ROWS:
        cells = spectra.reshape(local_blocks, pair_size, lag_size, share, width)
        cells = lax.dynamic_index_in_dim(cells, lax.axis_index("lag"), 2, keepdims=False)
        moved = lax.all_to_all(cells, "pair", 1, 1, tiled=True).reshape(blocks, share, width)
        rows = -(-share // ROWS) * ROWS
        return pl.pallas_call(
            whiten_kernel,
            out_shape=jax.ShapeDtypeStruct((blocks + 1, rows, width), jnp.bfloat16),
            in_specs=[vmem],
            out_specs=vmem,
            compiler_params=pltpu.CompilerParams(**params),
        )(jnp.pad(moved, ((0, 0), (0, rows - share), (0, 0))))
    white = pl.pallas_call(
        functools.partial(spread_kernel, pair_size, lag_size, share),
        out_shape=jax.ShapeDtypeStruct((local_blocks + 1, pair_size, share, width), jnp.bfloat16),
        in_specs=[pl.BlockSpec(memory_space=pltpu.HBM)],
        out_specs=vmem,
        scratch_shapes=[
            pltpu.VMEM((pair_size, local_blocks, share, width), spectra.dtype),
            pltpu.VMEM((width // 2, width // 2), jnp.bfloat16),
        ]
        + semaphores((pair_size - 1) * CHUNKS),
        compiler_params=pltpu.CompilerParams(collective_id=0, has_side_effects=True, **params),
    )(spectra)
    return white.reshape(blocks + pair_size, share, width)


def place(stacks, pair_size, lag_size, share):
    size = pair_size * lag_size
    groups, _, lags = stacks.shape
    piece = lags // size
    if share % ROWS or piece % 128:
        return lax.all_to_all(stacks[:, :share], ("pair", "lag"), 2, 1, tiled=True)
    return pl.pallas_call(
        functools.partial(place_kernel, size, lag_size, share, piece),
        out_shape=jax.ShapeDtypeStruct((groups, size * share, piece), stacks.dtype),
        in_specs=[pl.BlockSpec(memory_space=pl.ANY)],
        out_specs=pl.BlockSpec(memory_space=pltpu.VMEM),
        scratch_shapes=semaphores(size - 1),
        compiler_params=pltpu.CompilerParams(collective_id=1, has_side_effects=True),
    )(stacks)


def shards(spectra, pair_blocks, live_pairs, stack_group):
    pair_size = lax.axis_size("pair")
    lag_size = lax.axis_size("lag")
    _, _, channels, width = spectra.shape
    share = channels // (pair_size * lag_size)
    owners, slots = stack_group.shape
    even, odd = tables(width // 2)
    if share == ROWS and width == 8 * COLS and pair_size == 4 and lag_size == 2:
        pairs = pair_blocks.transpose(0, 2, 1)
        return fused(
            spectra, pairs, live_pairs, stack_group, even, odd, pair_size, lag_size, share
        )
    white = spread(spectra, pair_size, lag_size, share)
    rows = white.shape[1]
    smem = pl.BlockSpec(memory_space=pltpu.SMEM)
    vmem = pl.BlockSpec(memory_space=pltpu.VMEM)
    ids = pltpu.SMEM((NGRP * (owners * slots + QUAD) + QUAD,), jnp.int32)
    quads = pltpu.SMEM((owners * slots // QUAD + NGRP + BATCH,), jnp.int32)
    stacks = pl.pallas_call(
        kernel,
        out_shape=jax.ShapeDtypeStruct((NGRP, rows, width), jnp.bfloat16),
        in_specs=[smem] * 3 + [vmem] * 3,
        out_specs=vmem,
        scratch_shapes=[
            pltpu.VMEM((BATCH * rows, width), jnp.bfloat16),
            pltpu.VMEM((3, NGRP * rows, width), jnp.float32),
            ids, ids, quads, quads,
            pltpu.SMEM((NGRP,), jnp.int32),
        ],
        compiler_params=pltpu.CompilerParams(vmem_limit_bytes=40 << 20),
    )(
        pair_blocks.transpose(0, 2, 1), live_pairs, stack_group, white, even, odd
    )
    return place(stacks, pair_size, lag_size, share).astype(jnp.float32)


def solution(mesh):
    return jax.shard_map(
        shards,
        mesh=mesh,
        in_specs=(P("win", "pair", "stk", None), P("win", None, None), P("win"), P("win", None)),
        out_specs=P("win", "stk", ("pair", "lag")),
        check_vma=False,
    )
```
